256 devices in a mesh: seq: 32 (over y, x, core), chan: 8 (over z).
Axes of the slice: x: 4, y: 4, z: 8, core: 2. Of those that a mesh axis runs over, the one named last changes fastest.
Arguments:
- outer_gate: bfloat16 [8192, 4096], P('seq', 'chan'), may hold values from -6 to 6
- inner_gate: bfloat16 [8192, 4096], P('seq', 'chan'), may hold values from -6 to 6
- signal: bfloat16 [8192, 4096], P('seq', 'chan'), may hold values from -6 to 6
- cotangent: bfloat16 [8192, 4096], P('seq', 'chan'), may hold values from -6 to 6
- filters: float32 [8192, 512], P('seq', 'chan'), may hold values from -1.1 to 1.1
Outputs:
- outer_grad: bfloat16 [8192, 4096], P('seq', 'chan')
- inner_grad: bfloat16 [8192, 4096], P('seq', 'chan')
- signal_grad: bfloat16 [8192, 4096], P('seq', 'chan')
- filter_grad: float32 [8192, 512], P('seq', 'chan')
The draws below stay inside these ranges and needn't reach their ends.
All inputs are finite; a program needn't handle non-finite values.
Results may differ from the reference program's by a relative error of at most 0.0012.
Values sent between devices are 32-bit elements; how exact they have to be, the bound alone decides.
No kernel may reach another device: no remote copies, remote signals or barrier semaphores. Data moves between devices by JAX's collectives and lax.ppermute only.
A program may use at most 128 MiB of HBM per device.

```python
import math
import jax
import jax.numpy as jnp
from jax import lax

CHANNELS = 4096
FILTERS = 512
SEQ = 8192


def draw_filters(key, part):
    key = jax.random.fold_in(key, 7)
    span_key, value_key = jax.random.split(key, 2)
    steps_index = jnp.arange(SEQ, dtype=jnp.float32)[:, None]
    lowest = math.log(30.0)
    highest = math.log(4.0 * SEQ)
    rough = jnp.clip(jax.random.normal(value_key, (SEQ, FILTERS), jnp.float32), -4.0, 4.0)
    spans = jnp.exp(jax.random.uniform(span_key, (1, FILTERS), jnp.float32, lowest, highest))
    ratio = jnp.exp(-2.0 / spans)
    normalize = jnp.sqrt((1.0 - ratio) / (1.0 - ratio ** SEQ))
    return rough * jnp.exp(-steps_index / spans) * normalize


def shard_levels(key, extent, cuts, smallest, top_value):
    def one(axis_at, blocks):
        heights = jax.random.uniform(jax.random.fold_in(jax.random.fold_in(key, 6), axis_at), (blocks,), jnp.float32, smallest / len(cuts), top_value / len(cuts))
        return jnp.repeat(jnp.exp(heights), extent[axis_at] // blocks).reshape((-1,) + (1,) * (len(extent) - axis_at - 1))

    gain = one(*cuts[0])
    for cut in cuts[1:]:
        gain = gain * one(*cut)
    return gain


def noise(own_key, dims, width, reach, shards=(), held_as=jnp.bfloat16):
    level = shard_levels(own_key, dims, shards, -0.22, 0.18) if shards else 1.0
    values = jax.random.normal(own_key, dims, jnp.float32) * width * level
    return jnp.minimum(jnp.maximum(values, -reach), reach).astype(held_as)


def setup_inputs(seed: int = 0) -> dict:
    keys = jax.random.split(jax.random.key(seed), 6)
    outer_gate = noise(keys[0], (SEQ, CHANNELS), 1.0, 6.0, ((0, 32), (1, 8)))
    inner_gate = noise(keys[1], (SEQ, CHANNELS), 1.0, 6.0, ((0, 32), (1, 8)))
    signal = noise(keys[2], (SEQ, CHANNELS), 1.0, 6.0, ((0, 32), (1, 8)))
    cotangent = noise(keys[3], (SEQ, CHANNELS), 1.0, 6.0, ((0, 32), (1, 8)))
    filters = draw_filters(jax.random.fold_in(keys[5], 71), 0)
    return {"outer_gate": outer_gate, "inner_gate": inner_gate, "signal": signal, "cotangent": cotangent, "filters": filters}


def reference(outer_gate, inner_gate, signal, cotangent, filters):
    length = SEQ
    period = 2 * length
    repeats = CHANNELS // FILTERS
    filter_spec = jnp.fft.rfft(filters.astype(jnp.float32), n=period, axis=0)

    def channel_block(accumulated, block_index):
        offset = (block_index * FILTERS).astype(jnp.int32)

        def columns(operand):
            return lax.dynamic_slice_in_dim(operand, offset, FILTERS, 1).astype(jnp.float32)
        outer_part = columns(outer_gate)
        inner_part = columns(inner_gate)
        signal_part = columns(signal)
        upstream = columns(cotangent)
        signal_in = inner_part * signal_part
        local_grad = upstream * outer_part
        signal_spec = jnp.fft.rfft(signal_in, n=period, axis=0)
        grad_spec = jnp.fft.rfft(local_grad, n=period, axis=0)
        convolved = jnp.fft.irfft(filter_spec * signal_spec, n=period, axis=0)[:length]
        back_grad = jnp.fft.irfft(grad_spec * jnp.conj(filter_spec), n=period, axis=0)[:length]
        filter_terms = jnp.fft.irfft(grad_spec * jnp.conj(signal_spec), n=period, axis=0)[:length]
        gradients = ((upstream * convolved).astype(jnp.bfloat16), (back_grad * signal_part).astype(jnp.bfloat16), (back_grad * inner_part).astype(jnp.bfloat16))
        return (accumulated + filter_terms, gradients)
    initial = jnp.zeros((length, FILTERS), jnp.float32)
    accumulated, stacks = lax.scan(channel_block, initial, jnp.arange(repeats, dtype=jnp.int32))

    def channel_major(stacked):
        return jnp.transpose(stacked, (1, 0, 2)).reshape(length, CHANNELS)
    return (channel_major(stacks[0]), channel_major(stacks[1]), channel_major(stacks[2]), accumulated * (1.0 / math.sqrt(length)))
```

```python
import math

import jax
import jax.numpy as jnp
import numpy as np
import ml_dtypes
from jax import lax
from jax.experimental import pallas as pl
from jax.experimental.pallas import tpu as pltpu
from jax.sharding import PartitionSpec as P

BF = jnp.bfloat16
F32 = jnp.float32

N = 8192
A = 64
B = 128
ROWS = 40
MEMBERS = 64
VMEM_LIMIT = 40 * 1024 * 1024


def two_parts(table):
    high = table.astype(ml_dtypes.bfloat16)
    low = (table - high.astype(np.float64)).astype(ml_dtypes.bfloat16)
    return high, low


def tables():
    order = np.array([2 * s + h for h in range(2) for s in range(32)])
    k1 = np.arange(A) - 0.25
    angle1 = 2 * np.pi / A * np.outer(k1, order)
    w1 = np.concatenate([np.cos(angle1), -np.sin(angle1)], axis=0)
    high, low = two_parts(w1)
    w1cat = np.concatenate([high, high, low], axis=1)
    v1 = np.concatenate([np.cos(angle1), -np.sin(angle1)], axis=0).T / N
    high, low = two_parts(v1)
    v1cat = np.concatenate([high, high, low], axis=1)
    angle2 = 2 * np.pi / B * np.outer(np.arange(B), np.arange(B))
    c, s = np.cos(angle2), np.sin(angle2)
    w2 = np.block([[c, -s], [s, c]])
    w2h, w2l = two_parts(w2)
    v2h, v2l = two_parts(w2.T)
    angle = 2 * np.pi / N * np.outer(k1, np.arange(B))
    twiddle = np.stack([np.cos(angle), np.sin(angle)]).astype(np.float32)
    return w1cat, w2h, w2l, twiddle, v2h, v2l, v1cat


def split(x):
    high = x.astype(BF)
    return high, (x - high.astype(F32)).astype(BF)


def dot(x, y):
    return jnp.dot(x, y, preferred_element_type=F32)


def first_stage(columns, w1, c, s):
    high, low = split(jnp.concatenate(columns, axis=1))
    out = dot(w1, jnp.concatenate([high, low, high], axis=0))
    pairs = []
    for i in range(len(columns)):
        re = out[:A, i * B : (i + 1) * B]
        im = out[A:, i * B : (i + 1) * B]
        pairs.append((re * c + im * s, im * c - re * s))
    return pairs


def second_stage(pairs, high_table, low_table):
    stacked = jnp.concatenate([jnp.concatenate(p, axis=1) for p in pairs], axis=0)
    high, low = split(stacked)
    return dot(high, high_table) + dot(low, high_table) + dot(high, low_table)


def last_stage(blocks, v1, c, s):
    re, im = [], []
    for block in blocks:
        qr, qi = block[:, :B], block[:, B:]
        re.append(qr * c - qi * s)
        im.append(qr * s + qi * c)
    both = jnp.concatenate([jnp.concatenate(re, axis=1), jnp.concatenate(im, axis=1)], axis=0)
    high, low = split(both)
    return dot(v1, jnp.concatenate([high, low, high], axis=0))


def forward(columns, w1, w2h, w2l, c, s):
    return second_stage(first_stage(columns, w1, c, s), w2h, w2l)


def prep_kernel(outer_ref, inner_ref, signal_ref, cot_ref, filt_ref, send_ref):
    def place(block, first_row, h, cb):
        turned = block.T
        for e in range(2):
            row = first_row + h * 8 + cb * 2 + e
            send_ref[pl.ds(row, MEMBERS, stride=ROWS), :] = turned[e * 64 : (e + 1) * 64]

    for h in range(2):
        rows = slice(h * B, (h + 1) * B)
        for cb in range(4):
            cols = slice(cb * 128, (cb + 1) * 128)
            place(inner_ref[rows, cols].astype(F32) * signal_ref[rows, cols].astype(F32), 0, h, cb)
            place(cot_ref[rows, cols].astype(F32) * outer_ref[rows, cols].astype(F32), 16, h, cb)
        send_ref[pl.ds(32 + h, MEMBERS, stride=ROWS), :] = filt_ref[rows, :].T
    for row in range(34, ROWS):
        send_ref[pl.ds(row, MEMBERS, stride=ROWS), :] = jnp.zeros((MEMBERS, B), F32)


def gather_rows(ref, q, row):
    return jnp.concatenate(
        [ref[pl.ds(q * 32 * ROWS + row + 8 * h, 32, stride=ROWS), :] for h in range(2)], axis=0
    )


def pick_kernel(recv_ref, out_ref):
    for q in range(2):
        for h in range(2):
            block = recv_ref[pl.ds(q * 32 * ROWS + 32 + h, 32, stride=ROWS), :]
            for p in range(4):
                out_ref[p, q, h * 32 : (h + 1) * 32, :] = block


def spectra_kernel(recv_ref, w1_ref, w2h_ref, w2l_ref, tw_ref, v2h_ref, v2l_ref, v1_ref,
                   u_ref, g_ref, fg_ref, prod_ref):
    c, s = tw_ref[0], tw_ref[1]

    def step(f, carry):
        columns = [gather_rows(recv_ref, q, f + base) for base in (0, 16) for q in range(2)]
        spec = forward(columns, w1_ref[...], w2h_ref[...], w2l_ref[...], c, s)
        u_ref[f] = spec[: 2 * A]
        g_ref[f] = spec[2 * A :]
        ur, ui = spec[: 2 * A, :B], spec[: 2 * A, B:]
        gr, gi = spec[2 * A :, :B], spec[2 * A :, B:]
        pr = gr * ur + gi * ui
        pi = gi * ur - gr * ui
        prod_ref[f] = jnp.concatenate([pr[:A] + pr[A:], pi[:A] + pi[A:]], axis=1)
        return carry

    lax.fori_loop(0, 8, step, 0)

    def back(j, carry):
        prod = prod_ref[pl.ds(j * 4, 4)].reshape(4 * A, 2 * B)
        high, low = split(prod)
        mid = dot(high, v2h_ref[...]) + dot(low, v2h_ref[...]) + dot(high, v2l_ref[...])
        out = last_stage([mid[i * A : (i + 1) * A] for i in range(4)], v1_ref[...], c, s)
        for i in range(4):
            fg_ref[j * 2 + i // 2, i % 2] = out[:, i * B : (i + 1) * B]
        return carry

    lax.fori_loop(0, 2, back, 0)


def conv_kernel(filt_ref, u_ref, g_ref, w1_ref, w2h_ref, w2l_ref, tw_ref, v2h_ref, v2l_ref, v1_ref,
                out_ref, spec_ref):
    c, s = tw_ref[0], tw_ref[1]

    def filters(j, carry):
        columns = [filt_ref[j * 2 + i // 2, i % 2] for i in range(4)]
        spec = forward(columns, w1_ref[...], w2h_ref[...], w2l_ref[...], c, s)
        spec_ref[pl.ds(j * 4, 4)] = spec.reshape(4, A, 2 * B)
        return carry

    lax.fori_loop(0, 2, filters, 0)

    def step(f, carry):
        hr, hi = spec_ref[f][:, :B], spec_ref[f][:, B:]
        prods = []
        for q in range(2):
            ur, ui = u_ref[f, q * A : (q + 1) * A, :B], u_ref[f, q * A : (q + 1) * A, B:]
            prods.append((hr * ur - hi * ui, hr * ui + hi * ur))
        for q in range(2):
            gr, gi = g_ref[f, q * A : (q + 1) * A, :B], g_ref[f, q * A : (q + 1) * A, B:]
            prods.append((gr * hr + gi * hi, gi * hr - gr * hi))
        mid = second_stage(prods, v2h_ref[...], v2l_ref[...])
        out = last_stage([mid[i * A : (i + 1) * A] for i in range(4)], v1_ref[...], c, s)
        for i in range(4):
            q, base = i % 2, (i // 2) * 16
            for h in range(2):
                out_ref[pl.ds(q * 32 * ROWS + base + 8 * h + f, 32, stride=ROWS), :] = (
                    out[h * 32 : (h + 1) * 32, i * B : (i + 1) * B]
                )
        return carry

    lax.fori_loop(0, 8, step, 0)
    for row in range(34, ROWS):
        out_ref[pl.ds(row, MEMBERS, stride=ROWS), :] = jnp.zeros((MEMBERS, B), F32)


def place_kernel(fg_ref, base_ref, out_ref):
    out_ref[...] = base_ref[...]
    total = (fg_ref[0] + fg_ref[1]) + (fg_ref[2] + fg_ref[3])
    for q in range(2):
        for h in range(2):
            out_ref[pl.ds(q * 32 * ROWS + 32 + h, 32, stride=ROWS), :] = total[q, h * 32 : (h + 1) * 32]


def post_kernel(recv_ref, inner_ref, signal_ref, cot_ref, og_ref, ig_ref, sg_ref, fg_ref):
    def fetch(first_row, h, cb):
        blocks = [
            recv_ref[pl.ds(first_row + h * 8 + cb * 2 + e, MEMBERS, stride=ROWS), :] for e in range(2)
        ]
        return jnp.concatenate(blocks, axis=0).T

    for h in range(2):
        rows = slice(h * B, (h + 1) * B)
        for cb in range(4):
            cols = slice(cb * 128, (cb + 1) * 128)
            og_ref[rows, cols] = (cot_ref[rows, cols].astype(F32) * fetch(0, h, cb)).astype(BF)
            back = fetch(16, h, cb)
            ig_ref[rows, cols] = (back * signal_ref[rows, cols].astype(F32)).astype(BF)
            sg_ref[rows, cols] = (back * inner_ref[rows, cols].astype(F32)).astype(BF)
        block = recv_ref[pl.ds(32 + h, MEMBERS, stride=ROWS), :]
        fg_ref[rows, :] = block.T * (1.0 / math.sqrt(N))


def call(kernel, out_shapes, name, scratch=(), cost=(0, 0)):
    return pl.pallas_call(
        kernel,
        out_shape=out_shapes,
        scratch_shapes=list(scratch),
        name=name,
        compiler_params=pltpu.CompilerParams(vmem_limit_bytes=VMEM_LIMIT),
        cost_estimate=pl.CostEstimate(flops=cost[0], bytes_accessed=cost[1], transcendentals=0),
    )


def shape(*dims, dtype=F32):
    return jax.ShapeDtypeStruct(dims, dtype)


GROUPS = [[s * 8 + 2 * p + q for q in range(2) for s in range(32)] for p in range(4)]
QUADS = [[0, 2, 4, 6], [1, 3, 5, 7]]


def exchange(x):
    x = x.reshape(MEMBERS, ROWS, B)
    x = lax.all_to_all(x, ("seq", "chan"), 0, 0, axis_index_groups=GROUPS, tiled=True)
    return x.reshape(MEMBERS * ROWS, B)


def quad_exchange(x):
    return lax.all_to_all(x, "chan", 0, 0, axis_index_groups=QUADS, tiled=True)


def body(outer_gate, inner_gate, signal, cotangent, filters):
    consts = [jnp.asarray(t) for t in tables()]
    w1, w2h, w2l, tw, v2h, v2l, v1 = consts
    buffer = shape(MEMBERS * ROWS, B)
    send = call(prep_kernel, buffer, "prep")(outer_gate, inner_gate, signal, cotangent, filters)
    recv = exchange(send)
    picked = call(pick_kernel, shape(4, 2, A, B), "pick")(recv)
    gathered = quad_exchange(picked)
    u, g, fg = call(
        spectra_kernel,
        (shape(8, 2 * A, 2 * B), shape(8, 2 * A, 2 * B), shape(4, 2, A, B)),
        "spectra",
        [pltpu.VMEM((8, A, 2 * B), F32)],
        (2_000_000_000, 4_000_000),
    )(recv, w1, w2h, w2l, tw, v2h, v2l, v1)
    fg_parts = quad_exchange(fg)
    out = call(
        conv_kernel, buffer, "conv", [pltpu.VMEM((8, A, 2 * B), F32)], (2_000_000_000, 4_000_000)
    )(gathered, u, g, w1, w2h, w2l, tw, v2h, v2l, v1)
    back_send = call(place_kernel, buffer, "place")(fg_parts, out)
    landed = exchange(back_send)
    return call(
        post_kernel,
        (shape(256, 512, dtype=BF), shape(256, 512, dtype=BF), shape(256, 512, dtype=BF), shape(256, 64)),
        "post",
    )(landed, inner_gate, signal, cotangent)


def solution(mesh):
    spec = P("seq", "chan")
    return jax.shard_map(
        body, mesh=mesh, in_specs=(spec,) * 5, out_specs=(spec,) * 4, check_vma=False
    )
```

```python
import math

import jax
import jax.numpy as jnp
import numpy as np
import ml_dtypes
from jax import lax
from jax.experimental import pallas as pl
from jax.experimental.pallas import tpu as pltpu
from jax.sharding import PartitionSpec as P

BF = jnp.bfloat16
F32 = jnp.float32

N = 8192
A = 64
B = 128
SHARDS = 32
MEMBERS = 64
ROWS = 40
SCATTER = np.random.RandomState(0).permutation(SHARDS)
VMEM_LIMIT = 16 * 1024 * 1024


def two_parts(table):
    high = table.astype(ml_dtypes.bfloat16)
    low = (table - high.astype(np.float64)).astype(ml_dtypes.bfloat16)
    return high, low


def tables():
    order = np.array([2 * s + h for h in range(2) for s in SCATTER])
    k1 = np.arange(A) - 0.25
    angle1 = 2 * np.pi / A * np.outer(k1, order)
    w1 = np.concatenate([np.cos(angle1), -np.sin(angle1)], axis=0)
    high, low = two_parts(w1)
    w1cat = np.concatenate([high, high, low], axis=1)
    v1 = np.concatenate([np.cos(angle1), -np.sin(angle1)], axis=0).T / N
    high, low = two_parts(v1)
    v1cat = np.concatenate([high, high, low], axis=1)
    angle2 = 2 * np.pi / B * np.outer(np.arange(B), np.arange(B))
    c, s = np.cos(angle2), np.sin(angle2)
    w2 = np.block([[c, -s], [s, c]])
    w2h, w2l = two_parts(w2)
    v2h, v2l = two_parts(w2.T)
    angle = 2 * np.pi / N * np.outer(k1, np.arange(B))
    twiddle = np.stack([np.cos(angle), np.sin(angle)]).astype(np.float32)
    return w1cat, w2h, w2l, twiddle, v2h, v2l, v1cat


def split(x):
    high = x.astype(BF)
    return high, (x - high.astype(F32)).astype(BF)


def dot(x, y):
    return jnp.dot(x, y, preferred_element_type=F32)


def first_stage(columns, w1, c, s):
    high, low = split(jnp.concatenate(columns, axis=1))
    out = dot(w1, jnp.concatenate([high, low, high], axis=0))
    pairs = []
    for i in range(len(columns)):
        re = out[:A, i * B : (i + 1) * B]
        im = out[A:, i * B : (i + 1) * B]
        pairs.append((re * c + im * s, im * c - re * s))
    return pairs


def second_stage(pairs, high_table, low_table):
    stacked = jnp.concatenate([jnp.concatenate(p, axis=1) for p in pairs], axis=0)
    high, low = split(stacked)
    return dot(high, high_table) + dot(low, high_table) + dot(high, low_table)


def last_stage(blocks, v1, c, s):
    re, im = [], []
    for block in blocks:
        qr, qi = block[:, :B], block[:, B:]
        re.append(qr * c - qi * s)
        im.append(qr * s + qi * c)
    both = jnp.concatenate([jnp.concatenate(re, axis=1), jnp.concatenate(im, axis=1)], axis=0)
    high, low = split(both)
    return dot(v1, jnp.concatenate([high, low, high], axis=0))


def forward(columns, w1, w2h, w2l, c, s):
    return second_stage(first_stage(columns, w1, c, s), w2h, w2l)


def prep_kernel(outer_hbm, inner_hbm, signal_hbm, cot_hbm, filt_hbm, send_ref,
                outer_ref, inner_ref, signal_ref, cot_ref, filt_ref, sems):
    def load(i, from_ref, to_ref, rows):
        copy = pltpu.make_async_copy(from_ref.at[rows], to_ref.at[rows], sems.at[i])
        copy.start()
        return copy

    halves = [pl.ds(0, B), pl.ds(B, B)]
    pairs = [(inner_hbm, inner_ref), (signal_hbm, signal_ref), (cot_hbm, cot_ref), (outer_hbm, outer_ref)]
    copies = [load(i * 4 + j, *pair, rows) for i, rows in enumerate(halves) for j, pair in enumerate(pairs)]
    last = load(8, filt_hbm, filt_ref, pl.ds(0, 64))

    def place(block, first_row, h, cb):
        turned = block.T
        for e in range(2):
            row = first_row + h * 8 + cb * 2 + e
            send_ref[pl.ds(row, MEMBERS, stride=ROWS), :] = turned[e * 64 : (e + 1) * 64]

    for row in range(34, ROWS):
        send_ref[pl.ds(row, MEMBERS, stride=ROWS), :] = jnp.zeros((MEMBERS, B), F32)
    for h in range(2):
        rows = slice(h * B, (h + 1) * B)
        for copy in copies[h * 4 : h * 4 + 4]:
            copy.wait()
        for cb in range(4):
            cols = slice(cb * 128, (cb + 1) * 128)
            place(inner_ref[rows, cols].astype(F32) * signal_ref[rows, cols].astype(F32), 0, h, cb)
            place(cot_ref[rows, cols].astype(F32) * outer_ref[rows, cols].astype(F32), 16, h, cb)
    last.wait()
    for h in range(2):
        send_ref[pl.ds(32 + h, MEMBERS, stride=ROWS), :] = filt_ref[:, h * B : (h + 1) * B]


def partners():
    pair = lax.axis_index("chan") // 2
    beside = pair + 1 - 2 * lax.rem(pair, 2)
    return [pair, beside, lax.rem(pair + 2, 4), lax.rem(beside + 2, 4)]


def pick_kernel(recv_ref, out_ref):
    for q in range(2):
        out_ref[q] = gather_rows(recv_ref, q, 32, 1)


def filter_kernel(f0_ref, f1_ref, f2_ref, f3_ref, w1_ref, w2h_ref, w2l_ref, tw_ref, spec_ref):
    c, s = tw_ref[0], tw_ref[1]
    refs = (f0_ref, f1_ref, f2_ref, f3_ref)
    owners = partners()
    for k in range(0, 4, 2):
        columns = [refs[k + j][q] for j in range(2) for q in range(2)]
        spec = forward(columns, w1_ref[...], w2h_ref[...], w2l_ref[...], c, s)
        for j in range(2):
            for q in range(2):
                part = (j * 2 + q) * A
                spec_ref[owners[k + j] * 2 + q] = spec[part : part + A]


def gather_rows(ref, q, row, step):
    return jnp.concatenate(
        [ref[pl.ds(q * 32 * ROWS + row + step * h, 32, stride=ROWS), :] for h in range(2)], axis=0
    )


def spectra_kernel(recv_ref, w1_ref, w2h_ref, w2l_ref, tw_ref, v2h_ref, v2l_ref, v1_ref,
                   u_ref, g_ref, fg0_ref, fg1_ref, fg2_ref, fg3_ref, prod_ref):
    fg_refs = (fg0_ref, fg1_ref, fg2_ref, fg3_ref)
    c, s = tw_ref[0], tw_ref[1]

    def step(f, carry):
        columns = [gather_rows(recv_ref, q, f + base, 8) for base in (0, 16) for q in range(2)]
        spec = forward(columns, w1_ref[...], w2h_ref[...], w2l_ref[...], c, s)
        u_ref[f] = spec[: 2 * A]
        g_ref[f] = spec[2 * A :]
        ur, ui = spec[: 2 * A, :B], spec[: 2 * A, B:]
        gr, gi = spec[2 * A :, :B], spec[2 * A :, B:]
        pr = gr * ur + gi * ui
        pi = gi * ur - gr * ui
        prod_ref[f] = jnp.concatenate([pr[:A] + pr[A:], pi[:A] + pi[A:]], axis=1)
        return carry

    lax.fori_loop(0, 8, step, 0)

    owners = partners()
    for k in (2, 0):
        prod = jnp.concatenate(
            [prod_ref[owners[k + j] * 2 + q] for j in range(2) for q in range(2)], axis=0
        )
        high, low = split(prod)
        mid = dot(high, v2h_ref[...]) + dot(low, v2h_ref[...]) + dot(high, v2l_ref[...])
        out = last_stage([mid[i * A : (i + 1) * A] for i in range(4)], v1_ref[...], c, s)
        for i in range(4):
            fg_refs[k + i // 2][i % 2] = out[:, i * B : (i + 1) * B]


def conv_kernel(spec_ref, u_ref, g_ref, tw_ref, v2h_ref, v2l_ref, v1_ref, out_ref):
    c, s = tw_ref[0], tw_ref[1]

    def step(f, carry):
        hr, hi = spec_ref[f][:, :B], spec_ref[f][:, B:]
        prods = []
        for q in range(2):
            ur, ui = u_ref[f, q * A : (q + 1) * A, :B], u_ref[f, q * A : (q + 1) * A, B:]
            prods.append((hr * ur - hi * ui, hr * ui + hi * ur))
        for q in range(2):
            gr, gi = g_ref[f, q * A : (q + 1) * A, :B], g_ref[f, q * A : (q + 1) * A, B:]
            prods.append((gr * hr + gi * hi, gi * hr - gr * hi))
        mid = second_stage(prods, v2h_ref[...], v2l_ref[...])
        out = last_stage([mid[i * A : (i + 1) * A] for i in range(4)], v1_ref[...], c, s)
        for i in range(4):
            q, base = i % 2, (i // 2) * 16
            for h in range(2):
                out_ref[pl.ds(q * 32 * ROWS + base + 8 * h + f, 32, stride=ROWS), :] = (
                    out[h * 32 : (h + 1) * 32, i * B : (i + 1) * B]
                )
        return carry

    lax.fori_loop(0, 8, step, 0)
    for row in range(34, ROWS):
        out_ref[pl.ds(row, MEMBERS, stride=ROWS), :] = jnp.zeros((MEMBERS, B), F32)


def place_kernel(fg0_ref, fg1_ref, fg2_ref, fg3_ref, base_ref, out_ref):
    total = (fg0_ref[...] + fg1_ref[...]) + (fg2_ref[...] + fg3_ref[...])
    for q in range(2):
        for h in range(2):
            out_ref[pl.ds(q * 32 * ROWS + 32 + h, 32, stride=ROWS), :] = total[q, h * 32 : (h + 1) * 32]


def post_kernel(recv_ref, inner_ref, signal_ref, cot_ref, og_ref, ig_ref, sg_ref, fg_ref):
    def fetch(first_row, h, cb):
        blocks = [
            recv_ref[pl.ds(first_row + h * 8 + cb * 2 + e, MEMBERS, stride=ROWS), :] for e in range(2)
        ]
        return jnp.concatenate(blocks, axis=0).T

    for h in range(2):
        rows = slice(h * B, (h + 1) * B)
        for cb in range(4):
            cols = slice(cb * 128, (cb + 1) * 128)
            og_ref[rows, cols] = (cot_ref[rows, cols].astype(F32) * fetch(0, h, cb)).astype(BF)
            back = fetch(16, h, cb)
            ig_ref[rows, cols] = (back * signal_ref[rows, cols].astype(F32)).astype(BF)
            sg_ref[rows, cols] = (back * inner_ref[rows, cols].astype(F32)).astype(BF)
        block = recv_ref[pl.ds(32 + h, MEMBERS, stride=ROWS), :]
        fg_ref[:, rows] = block * (1.0 / math.sqrt(N))


def call(kernel, out_shapes, name, scratch=(), cost=(0, 0), aliases=None, ins=None):
    return pl.pallas_call(
        kernel,
        out_shape=out_shapes,
        in_specs=pl.no_block_spec if ins is None else ins,
        scratch_shapes=list(scratch),
        name=name,
        input_output_aliases=aliases or {},
        compiler_params=pltpu.CompilerParams(vmem_limit_bytes=VMEM_LIMIT),
        cost_estimate=pl.CostEstimate(flops=cost[0], bytes_accessed=cost[1], transcendentals=0),
    )


def shape(*dims, dtype=F32):
    return jax.ShapeDtypeStruct(dims, dtype)


PAIRS = [[s * 8 + 2 * p + q for q in range(2) for s in SCATTER.tolist()] for p in range(4)]


def exchange(x):
    x = x.reshape(MEMBERS, ROWS, B)
    x = lax.all_to_all(x, ("seq", "chan"), 0, 0, axis_index_groups=PAIRS, tiled=True)
    return x.reshape(MEMBERS * ROWS, B)


def swap(x, distance):
    return lax.ppermute(x, "chan", [(z, z ^ distance) for z in range(8)])


def body(outer_gate, inner_gate, signal, cotangent, filters):
    w1, w2h, w2l, tw, v2h, v2l, v1 = [jnp.asarray(t) for t in tables()]
    buffer, spectra = shape(MEMBERS * ROWS, B), shape(8, A, 2 * B)
    two = shape(2, A, B)
    gate = pltpu.VMEM((256, 512), BF)
    send = call(
        prep_kernel, buffer, "prep",
        [gate, gate, gate, gate, pltpu.VMEM((64, 256), F32), pltpu.SemaphoreType.DMA((9,))],
        ins=[pl.BlockSpec(memory_space=pltpu.HBM)] * 5,
    )(*[
        pltpu.with_memory_space_constraint(x, pltpu.HBM)
        for x in (outer_gate, inner_gate, signal, cotangent, filters.T)
    ])
    recv = exchange(send)
    own = call(pick_kernel, two, "pick")(recv)
    f2, f1, f3 = [swap(own, d) for d in (4, 2, 6)]
    u, g, fg0, fg1, fg2, fg3 = call(
        spectra_kernel,
        (shape(8, 2 * A, 2 * B), shape(8, 2 * A, 2 * B), two, two, two, two),
        "spectra",
        [pltpu.VMEM((8, A, 2 * B), F32)],
        (2_000_000_000, 4_000_000),
    )(recv, w1, w2h, w2l, tw, v2h, v2l, v1)
    fg2, fg1, fg3 = [swap(x, d) for x, d in ((fg2, 4), (fg1, 2), (fg3, 6))]
    spec = call(filter_kernel, spectra, "filters", cost=(500_000_000, 1_000_000))(
        own, f1, f2, f3, w1, w2h, w2l, tw
    )
    out = call(conv_kernel, buffer, "conv", cost=(2_000_000_000, 4_000_000))(
        spec, u, g, tw, v2h, v2l, v1
    )
    back_send = call(place_kernel, buffer, "place", aliases={4: 0})(fg0, fg1, fg2, fg3, out)
    landed = exchange(back_send)
    *grads, fg = call(
        post_kernel,
        (shape(256, 512, dtype=BF), shape(256, 512, dtype=BF), shape(256, 512, dtype=BF), shape(64, 256)),
        "post",
    )(landed, inner_gate, signal, cotangent)
    return (*grads, fg.T)


def solution(mesh):
    spec = P("seq", "chan")
    return jax.shard_map(
        body, mesh=mesh, in_specs=(spec,) * 5, out_specs=(spec,) * 4, check_vma=False
    )
```

```python
import math

import jax
import jax.numpy as jnp
import numpy as np
import ml_dtypes
from jax import lax
from jax.experimental import pallas as pl
from jax.experimental.pallas import tpu as pltpu
from jax.sharding import PartitionSpec as P

BF = jnp.bfloat16
F32 = jnp.float32

N = 8192
A = 64
B = 128
SHARDS = 32
MEMBERS = 64
ROWS = 34
SCATTER = np.random.RandomState(0).permutation(SHARDS)
VMEM_LIMIT = 16 * 1024 * 1024


def two_parts(table):
    high = table.astype(ml_dtypes.bfloat16)
    low = (table - high.astype(np.float64)).astype(ml_dtypes.bfloat16)
    return high, low


def tables():
    order = np.array([2 * s + h for h in range(2) for s in SCATTER])
    k1 = np.arange(A) - 0.25
    angle1 = 2 * np.pi / A * np.outer(k1, order)
    w1 = np.concatenate([np.cos(angle1), -np.sin(angle1)], axis=0)
    high, low = two_parts(w1)
    w1cat = np.concatenate([high, high, low], axis=1)
    v1 = np.concatenate([np.cos(angle1), -np.sin(angle1)], axis=0).T / N
    high, low = two_parts(v1)
    v1cat = np.concatenate([high, high, low], axis=1)
    angle2 = 2 * np.pi / B * np.outer(np.arange(B), np.arange(B))
    c, s = np.cos(angle2), np.sin(angle2)
    w2 = np.block([[c, -s], [s, c]])
    w2h, w2l = two_parts(w2)
    v2h, v2l = two_parts(w2.T)
    angle = 2 * np.pi / N * np.outer(k1, np.arange(B))
    twiddle = np.stack([np.cos(angle), np.sin(angle)]).astype(np.float32)
    return w1cat, w2h, w2l, twiddle, v2h, v2l, v1cat


def split(x):
    high = x.astype(BF)
    return high, (x - high.astype(F32)).astype(BF)


def dot(x, y):
    return jnp.dot(x, y, preferred_element_type=F32)


def first_stage(columns, w1, c, s):
    high, low = split(jnp.concatenate(columns, axis=1))
    out = dot(w1, jnp.concatenate([high, low, high], axis=0))
    pairs = []
    for i in range(len(columns)):
        re = out[:A, i * B : (i + 1) * B]
        im = out[A:, i * B : (i + 1) * B]
        pairs.append((re * c + im * s, im * c - re * s))
    return pairs


def second_stage(pairs, high_table, low_table):
    stacked = jnp.concatenate([jnp.concatenate(p, axis=1) for p in pairs], axis=0)
    high, low = split(stacked)
    return dot(high, high_table) + dot(low, high_table) + dot(high, low_table)


def last_stage(blocks, v1, c, s):
    re, im = [], []
    for block in blocks:
        qr, qi = block[:, :B], block[:, B:]
        re.append(qr * c - qi * s)
        im.append(qr * s + qi * c)
    both = jnp.concatenate([jnp.concatenate(re, axis=1), jnp.concatenate(im, axis=1)], axis=0)
    high, low = split(both)
    vh, vl = v1[:, : 2 * A], v1[:, 4 * A :]
    return dot(v1[:, : 4 * A], jnp.concatenate([high, low], axis=0)) + dot(vl, high)


def forward(columns, w1, w2h, w2l, c, s):
    return second_stage(first_stage(columns, w1, c, s), w2h, w2l)


def prep_kernel(outer_hbm, inner_hbm, signal_hbm, cot_hbm, filt_hbm, send_ref,
                outer_ref, inner_ref, signal_ref, cot_ref, filt_ref, sems):
    def load(i, from_ref, to_ref, rows):
        copy = pltpu.make_async_copy(from_ref.at[rows], to_ref.at[rows], sems.at[i])
        copy.start()
        return copy

    halves = [pl.ds(0, B), pl.ds(B, B)]
    pairs = [(inner_hbm, inner_ref), (signal_hbm, signal_ref), (cot_hbm, cot_ref), (outer_hbm, outer_ref)]
    copies = [load(i * 4 + j, *pair, rows) for i, rows in enumerate(halves) for j, pair in enumerate(pairs)]
    last = load(8, filt_hbm, filt_ref, pl.ds(0, 64))

    def place(block, first_row, h, cb):
        turned = block.T
        for e in range(2):
            row = first_row + h * 8 + cb * 2 + e
            send_ref[pl.ds(row, MEMBERS, stride=ROWS), :] = turned[e * 64 : (e + 1) * 64]

    for h in range(2):
        rows = slice(h * B, (h + 1) * B)
        for copy in copies[h * 4 : h * 4 + 4]:
            copy.wait()
        for cb in range(4):
            cols = slice(cb * 128, (cb + 1) * 128)
            place(inner_ref[rows, cols].astype(F32) * signal_ref[rows, cols].astype(F32), 0, h, cb)
            place(cot_ref[rows, cols].astype(F32) * outer_ref[rows, cols].astype(F32), 16, h, cb)
    last.wait()
    for h in range(2):
        send_ref[pl.ds(32 + h, MEMBERS, stride=ROWS), :] = filt_ref[:, h * B : (h + 1) * B]


def partners():
    pair = lax.axis_index("chan") // 2
    beside = pair + 1 - 2 * lax.rem(pair, 2)
    return [pair, beside, lax.rem(pair + 2, 4), lax.rem(beside + 2, 4)]


def pick_kernel(recv_ref, out_ref):
    for q in range(2):
        out_ref[q] = gather_rows(recv_ref, q, 32, 1)


def filter_kernel(f0_ref, f1_ref, f2_ref, f3_ref, w1_ref, w2h_ref, w2l_ref, tw_ref, spec_ref):
    c, s = tw_ref[0], tw_ref[1]
    refs = (f0_ref, f1_ref, f2_ref, f3_ref)
    owners = partners()
    for k in range(0, 4, 2):
        columns = [refs[k + j][q] for j in range(2) for q in range(2)]
        spec = forward(columns, w1_ref[...], w2h_ref[...], w2l_ref[...], c, s)
        for j in range(2):
            for q in range(2):
                part = (j * 2 + q) * A
                spec_ref[owners[k + j] * 2 + q] = spec[part : part + A]


def gather_rows(ref, q, row, step):
    return jnp.concatenate(
        [ref[pl.ds(q * 32 * ROWS + row + step * h, 32, stride=ROWS), :] for h in range(2)], axis=0
    )


def spectra_kernel(recv_ref, w1_ref, w2h_ref, w2l_ref, tw_ref, v2h_ref, v2l_ref, v1_ref,
                   u_ref, g_ref, fg0_ref, fg1_ref, fg2_ref, fg3_ref, prod_ref):
    fg_refs = (fg0_ref, fg1_ref, fg2_ref, fg3_ref)
    c, s = tw_ref[0], tw_ref[1]

    def step(f, carry):
        columns = [gather_rows(recv_ref, q, f + base, 8) for base in (0, 16) for q in range(2)]
        spec = forward(columns, w1_ref[...], w2h_ref[...], w2l_ref[...], c, s)
        u_ref[f] = spec[: 2 * A]
        g_ref[f] = spec[2 * A :]
        ur, ui = spec[: 2 * A, :B], spec[: 2 * A, B:]
        gr, gi = spec[2 * A :, :B], spec[2 * A :, B:]
        pr = gr * ur + gi * ui
        pi = gi * ur - gr * ui
        prod_ref[f] = jnp.concatenate([pr[:A] + pr[A:], pi[:A] + pi[A:]], axis=1)
        return carry

    lax.fori_loop(0, 8, step, 0, unroll=True)

    owners = partners()
    for k in (2, 0):
        prod = jnp.concatenate(
            [prod_ref[owners[k + j] * 2 + q] for j in range(2) for q in range(2)], axis=0
        )
        high, low = split(prod)
        mid = dot(high, v2h_ref[...]) + dot(low, v2h_ref[...]) + dot(high, v2l_ref[...])
        out = last_stage([mid[i * A : (i + 1) * A] for i in range(4)], v1_ref[...], c, s)
        for i in range(4):
            fg_refs[k + i // 2][i % 2] = out[:, i * B : (i + 1) * B]


def conv_kernel(spec_ref, u_ref, g_ref, tw_ref, v2h_ref, v2l_ref, v1_ref, out_ref):
    c, s = tw_ref[0], tw_ref[1]

    def step(f, carry):
        hr, hi = spec_ref[f][:, :B], spec_ref[f][:, B:]
        prods = []
        for q in range(2):
            ur, ui = u_ref[f, q * A : (q + 1) * A, :B], u_ref[f, q * A : (q + 1) * A, B:]
            prods.append((hr * ur - hi * ui, hr * ui + hi * ur))
        for q in range(2):
            gr, gi = g_ref[f, q * A : (q + 1) * A, :B], g_ref[f, q * A : (q + 1) * A, B:]
            prods.append((gr * hr + gi * hi, gi * hr - gr * hi))
        mid = second_stage(prods, v2h_ref[...], v2l_ref[...])
        out = last_stage([mid[i * A : (i + 1) * A] for i in range(4)], v1_ref[...], c, s)
        for i in range(4):
            q, base = i % 2, (i // 2) * 16
            for h in range(2):
                out_ref[pl.ds(q * 32 * ROWS + base + 8 * h + f, 32, stride=ROWS), :] = (
                    out[h * 32 : (h + 1) * 32, i * B : (i + 1) * B]
                )
        return carry

    lax.fori_loop(0, 8, step, 0, unroll=True)


def place_kernel(fg0_ref, fg1_ref, fg2_ref, fg3_ref, base_ref, out_ref):
    out_ref[...] = base_ref[...]
    total = (fg0_ref[...] + fg1_ref[...]) + (fg2_ref[...] + fg3_ref[...])
    for q in range(2):
        for h in range(2):
            out_ref[pl.ds(q * 32 * ROWS + 32 + h, 32, stride=ROWS), :] = total[q, h * 32 : (h + 1) * 32]


def post_kernel(recv_ref, inner_ref, signal_ref, cot_ref, og_hbm, ig_hbm, sg_hbm, fg_hbm,
                og_ref, ig_ref, sg_ref, fg_ref, sems):
    def fetch(first_row, h, cb):
        blocks = [
            recv_ref[pl.ds(first_row + h * 8 + cb * 2 + e, MEMBERS, stride=ROWS), :] for e in range(2)
        ]
        return jnp.concatenate(blocks, axis=0).T

    copies = []

    def store(from_ref, to_ref, rows):
        copy = pltpu.make_async_copy(from_ref.at[rows], to_ref.at[rows], sems.at[len(copies)])
        copy.start()
        copies.append(copy)

    for h in range(2):
        block = recv_ref[pl.ds(32 + h, MEMBERS, stride=ROWS), :]
        fg_ref[:, h * B : (h + 1) * B] = block * (1.0 / math.sqrt(N))
    store(fg_ref, fg_hbm, pl.ds(0, 64))
    for h in range(2):
        rows = slice(h * B, (h + 1) * B)
        for cb in range(4):
            cols = slice(cb * 128, (cb + 1) * 128)
            og_ref[rows, cols] = (cot_ref[rows, cols].astype(F32) * fetch(0, h, cb)).astype(BF)
        store(og_ref, og_hbm, pl.ds(h * B, B))
        for cb in range(4):
            cols = slice(cb * 128, (cb + 1) * 128)
            back = fetch(16, h, cb)
            ig_ref[rows, cols] = (back * signal_ref[rows, cols].astype(F32)).astype(BF)
            sg_ref[rows, cols] = (back * inner_ref[rows, cols].astype(F32)).astype(BF)
        store(ig_ref, ig_hbm, pl.ds(h * B, B))
        store(sg_ref, sg_hbm, pl.ds(h * B, B))
    for copy in copies:
        copy.wait()


def call(kernel, out_shapes, name, scratch=(), cost=(0, 0), ins=None, outs=None):
    return pl.pallas_call(
        kernel,
        out_shape=out_shapes,
        in_specs=pl.no_block_spec if ins is None else ins,
        scratch_shapes=list(scratch),
        name=name,
        out_specs=pl.no_block_spec if outs is None else outs,
        compiler_params=pltpu.CompilerParams(vmem_limit_bytes=VMEM_LIMIT),
        cost_estimate=pl.CostEstimate(flops=cost[0], bytes_accessed=cost[1], transcendentals=0),
    )


def shape(*dims, dtype=F32):
    return jax.ShapeDtypeStruct(dims, dtype)


PAIRS = [[s * 8 + 2 * p + q for q in range(2) for s in SCATTER.tolist()] for p in range(4)]


def exchange(x):
    x = x.reshape(MEMBERS, ROWS * B)
    x = lax.all_to_all(x, ("seq", "chan"), 0, 0, axis_index_groups=PAIRS, tiled=True)
    return x.reshape(MEMBERS * ROWS, B)


def swap(x, distance):
    return lax.ppermute(x, "chan", [(z, z ^ distance) for z in range(8)])


def body(outer_gate, inner_gate, signal, cotangent, filters):
    w1, w2h, w2l, tw, v2h, v2l, v1 = [jnp.asarray(t) for t in tables()]
    buffer, spectra = shape(MEMBERS * ROWS, B), shape(8, A, 2 * B)
    two = shape(2, A, B)
    gate = pltpu.VMEM((256, 512), BF)
    send = call(
        prep_kernel, buffer, "prep",
        [gate, gate, gate, gate, pltpu.VMEM((64, 256), F32), pltpu.SemaphoreType.DMA((9,))],
        ins=[pl.BlockSpec(memory_space=pltpu.HBM)] * 5,
    )(*[
        pltpu.with_memory_space_constraint(x, pltpu.HBM)
        for x in (outer_gate, inner_gate, signal, cotangent, filters.T)
    ])
    recv = exchange(send)
    own = call(pick_kernel, two, "pick")(recv)
    f2, f1, f3 = [swap(own, d) for d in (4, 2, 6)]
    u, g, fg0, fg1, fg2, fg3 = call(
        spectra_kernel,
        (shape(8, 2 * A, 2 * B), shape(8, 2 * A, 2 * B), two, two, two, two),
        "spectra",
        [pltpu.VMEM((8, A, 2 * B), F32)],
        (2_000_000_000, 4_000_000),
    )(recv, w1, w2h, w2l, tw, v2h, v2l, v1)
    fg2, fg1, fg3 = [swap(x, d) for x, d in ((fg2, 4), (fg1, 2), (fg3, 6))]
    spec = call(filter_kernel, spectra, "filters", cost=(500_000_000, 1_000_000))(
        own, f1, f2, f3, w1, w2h, w2l, tw
    )
    out = call(conv_kernel, buffer, "conv", cost=(2_000_000_000, 4_000_000))(
        spec, u, g, tw, v2h, v2l, v1
    )
    back_send = call(place_kernel, buffer, "place")(fg0, fg1, fg2, fg3, out)
    landed = exchange(back_send)
    *grads, fg = call(
        post_kernel,
        (shape(256, 512, dtype=BF), shape(256, 512, dtype=BF), shape(256, 512, dtype=BF), shape(64, 256)),
        "post",
        [gate, gate, gate, pltpu.VMEM((64, 256), F32), pltpu.SemaphoreType.DMA((7,))],
        outs=[pl.BlockSpec(memory_space=pltpu.HBM)] * 4,
    )(landed, inner_gate, signal, cotangent)
    return (*grads, fg.T)


def solution(mesh):
    spec = P("seq", "chan")
    return jax.shard_map(
        body, mesh=mesh, in_specs=(spec,) * 5, out_specs=(spec,) * 4, check_vma=False
    )
```

```python
import functools
import math

import jax
import jax.numpy as jnp
import numpy as np
import ml_dtypes
from jax import lax
from jax.experimental import pallas as pl
from jax.experimental.pallas import tpu as pltpu
from jax.sharding import PartitionSpec as P

BF = jnp.bfloat16
F32 = jnp.float32

N = 8192
A = 64
B = 128
SHARDS = 32
MEMBERS = 64
ROWS = 34
SCATTER = np.random.RandomState(0).permutation(SHARDS)
VMEM_LIMIT = 16 * 1024 * 1024


def two_parts(table):
    high = table.astype(ml_dtypes.bfloat16)
    low = (table - high.astype(np.float64)).astype(ml_dtypes.bfloat16)
    return high, low


def tables():
    order = np.array([2 * s + h for h in range(2) for s in SCATTER])
    k1 = np.arange(A) - 0.25
    angle1 = 2 * np.pi / A * np.outer(k1, order)
    w1 = np.concatenate([np.cos(angle1), -np.sin(angle1)], axis=0)
    high, low = two_parts(w1)
    w1cat = np.concatenate([high, high, low], axis=1)
    v1 = np.concatenate([np.cos(angle1), -np.sin(angle1)], axis=0).T / N
    high, low = two_parts(v1)
    v1cat = np.concatenate([high, high, low], axis=1)
    angle2 = 2 * np.pi / B * np.outer(np.arange(B), np.arange(B))
    c, s = np.cos(angle2), np.sin(angle2)
    w2 = np.block([[c, -s], [s, c]])
    w2h, w2l = two_parts(w2)
    angle = 2 * np.pi / N * np.outer(k1, np.arange(B))
    twiddle = np.stack([np.cos(angle), np.sin(angle)]).astype(np.float32)
    return w1cat, w2h, w2l, twiddle, v1cat


def split(x):
    high = x.astype(BF)
    return high, (x - high.astype(F32)).astype(BF)


def dot(x, y):
    return jnp.dot(x, y, preferred_element_type=F32)


def first_stage(columns, w1, c, s):
    high, low = split(jnp.concatenate(columns, axis=1))
    out = dot(w1, jnp.concatenate([high, low, high], axis=0))
    pairs = []
    for i in range(len(columns)):
        re = out[:A, i * B : (i + 1) * B]
        im = out[A:, i * B : (i + 1) * B]
        pairs.append((re * c + im * s, im * c - re * s))
    return pairs


def second_stage(pairs, high_table, low_table):
    stacked = jnp.concatenate([jnp.concatenate(p, axis=1) for p in pairs], axis=0)
    high, low = split(stacked)
    return dot(high, high_table) + dot(low, high_table) + dot(high, low_table)


def last_stage(blocks, v1, c, s):
    re, im = [], []
    for block in blocks:
        qi, qr = block[:, :B], block[:, B:]
        re.append(qr * c - qi * s)
        im.append(qr * s + qi * c)
    both = jnp.concatenate([jnp.concatenate(re, axis=1), jnp.concatenate(im, axis=1)], axis=0)
    high, low = split(both)
    vh, vl = v1[:, : 2 * A], v1[:, 4 * A :]
    return dot(v1[:, : 4 * A], jnp.concatenate([high, low], axis=0)) + dot(vl, high)


def forward(columns, w1, w2h, w2l, c, s):
    return second_stage(first_stage(columns, w1, c, s), w2h, w2l)


def prep_kernel(outer_hbm, inner_hbm, signal_hbm, cot_hbm, filt_hbm, send_ref,
                outer_ref, inner_ref, signal_ref, cot_ref, filt_ref, sems):
    def load(i, from_ref, to_ref, rows):
        copy = pltpu.make_async_copy(from_ref.at[rows], to_ref.at[rows], sems.at[i])
        copy.start()
        return copy

    halves = [pl.ds(0, B), pl.ds(B, B)]
    arrays = [(inner_hbm, inner_ref), (signal_hbm, signal_ref), (cot_hbm, cot_ref), (outer_hbm, outer_ref)]
    copies = [load(i * 4 + j, *pair, rows) for i, rows in enumerate(halves) for j, pair in enumerate(arrays)]
    last = load(8, filt_hbm, filt_ref, pl.ds(0, 64))

    pairs = partners()

    def place(block, first_row, h, k):
        turned = block.T
        for e in range(2):
            row = first_row + h * 8 + k * 2 + e
            send_ref[pl.ds(row, MEMBERS, stride=ROWS), :] = turned[e * 64 : (e + 1) * 64]

    for h in range(2):
        rows = slice(h * B, (h + 1) * B)
        for copy in copies[h * 4 : h * 4 + 4]:
            copy.wait()
        for k in range(4):
            cols = pl.ds(pl.multiple_of(pairs[k] * B, B), B)
            place(inner_ref[rows, cols].astype(F32) * signal_ref[rows, cols].astype(F32), 0, h, k)
            place(cot_ref[rows, cols].astype(F32) * outer_ref[rows, cols].astype(F32), 16, h, k)
    last.wait()
    for h in range(2):
        send_ref[pl.ds(32 + h, MEMBERS, stride=ROWS), :] = filt_ref[:, h * B : (h + 1) * B]


def partners():
    pair = lax.axis_index("chan") // 2
    beside = pair + 1 - 2 * lax.rem(pair, 2)
    return [pair, beside, lax.rem(pair + 2, 4), lax.rem(beside + 2, 4)]


def gather_rows(ref, q, row, step):
    return jnp.concatenate(
        [ref[pl.ds(q * 32 * ROWS + row + step * h, 32, stride=ROWS), :] for h in range(2)], axis=0
    )


def pick_kernel(recv_ref, out_ref):
    for q in range(2):
        out_ref[q] = gather_rows(recv_ref, q, 32, 1)


def spectra_kernel(recv_ref, w1_ref, w2h_ref, w2l_ref, tw_ref, v1_ref, u_ref, g_ref, fg_ref,
                   prod_ref, *, first):
    c, s = tw_ref[0], tw_ref[1]
    for f in range(4):
        columns = [gather_rows(recv_ref, q, first + f + base, 8) for base in (0, 16) for q in range(2)]
        spec = forward(columns, w1_ref[...], w2h_ref[...], w2l_ref[...], c, s)
        u_ref[f] = spec[: 2 * A]
        g_ref[f] = spec[2 * A :]
        ur, ui = spec[: 2 * A, :B], spec[: 2 * A, B:]
        gr, gi = spec[2 * A :, :B], spec[2 * A :, B:]
        pr = gr * ur + gi * ui
        pi = gi * ur - gr * ui
        prod_ref[f] = jnp.concatenate([pi[:A] + pi[A:], pr[:A] + pr[A:]], axis=1)
    high, low = split(prod_ref[...].reshape(4 * A, 2 * B))
    mid = dot(high, w2h_ref[...]) + dot(low, w2h_ref[...]) + dot(high, w2l_ref[...])
    out = last_stage([mid[i * A : (i + 1) * A] for i in range(4)], v1_ref[...], c, s)
    for i in range(4):
        fg_ref[i] = out[:, i * B : (i + 1) * B]


def mix_kernel(near_ref, came_ref, keep_ref, give_ref):
    keep_ref[...] = near_ref[0:2] + came_ref[2:4]
    give_ref[...] = near_ref[2:4] + came_ref[0:2]


def conv_part(ks, filts, u_refs, g_refs, w1, w2h, w2l, tw_ref, v1, out_ref):
    c, s = tw_ref[0], tw_ref[1]
    spec = forward([filt[q] for filt in filts for q in range(2)], w1, w2h, w2l, c, s)
    for j, k in enumerate(ks):
        for e in range(2):
            f = 2 * k + e
            u_ref, g_ref, at = u_refs[k // 2], g_refs[k // 2], f % 4
            h_spec = spec[(2 * j + e) * A : (2 * j + e + 1) * A]
            hr, hi = h_spec[:, :B], h_spec[:, B:]
            prods = []
            for q in range(2):
                ur, ui = u_ref[at, q * A : (q + 1) * A, :B], u_ref[at, q * A : (q + 1) * A, B:]
                prods.append((hr * ui + hi * ur, hr * ur - hi * ui))
            for q in range(2):
                gr, gi = g_ref[at, q * A : (q + 1) * A, :B], g_ref[at, q * A : (q + 1) * A, B:]
                prods.append((gi * hr - gr * hi, gr * hr + gi * hi))
            mid = second_stage(prods, w2h, w2l)
            out = last_stage([mid[i * A : (i + 1) * A] for i in range(4)], v1, c, s)
            for i in range(4):
                q, base = i % 2, (i // 2) * 16
                for h in range(2):
                    out_ref[pl.ds(q * 32 * ROWS + base + 8 * h + f, 32, stride=ROWS), :] = (
                        out[h * 32 : (h + 1) * 32, i * B : (i + 1) * B]
                    )


def conv_even_kernel(own_ref, f3_ref, u0_ref, g0_ref, u1_ref, g1_ref, w1_ref, w2h_ref, w2l_ref, tw_ref, v1_ref,
                     out_ref):
    conv_part((0, 3), (own_ref, f3_ref), (u0_ref, u1_ref), (g0_ref, g1_ref), w1_ref[...], w2h_ref[...], w2l_ref[...], tw_ref,
              v1_ref[...], out_ref)


def conv_odd_kernel(far_ref, base_ref, u0_ref, g0_ref, u1_ref, g1_ref, w1_ref, w2h_ref, w2l_ref,
                    tw_ref, v1_ref, out_ref):
    out_ref[...] = base_ref[...]
    conv_part((1, 2), (far_ref.at[0], far_ref.at[1]), (u0_ref, u1_ref), (g0_ref, g1_ref), w1_ref[...], w2h_ref[...],
              w2l_ref[...], tw_ref, v1_ref[...], out_ref)


def place_kernel(keep_ref, came_ref, base_ref, out_ref):
    out_ref[...] = base_ref[...]
    for q in range(2):
        total = keep_ref[q] + came_ref[q]
        for h in range(2):
            out_ref[pl.ds(q * 32 * ROWS + 32 + h, 32, stride=ROWS), :] = total[h * 32 : (h + 1) * 32]


def post_kernel(recv_ref, inner_ref, signal_ref, cot_ref, og_hbm, ig_hbm, sg_hbm, fg_hbm,
                og_ref, ig_ref, sg_ref, fg_ref, sems):
    pairs = partners()

    def fetch(first_row, h, k):
        blocks = [
            recv_ref[pl.ds(first_row + h * 8 + k * 2 + e, MEMBERS, stride=ROWS), :] for e in range(2)
        ]
        return jnp.concatenate(blocks, axis=0).T

    copies = []

    def store(from_ref, to_ref, rows):
        copy = pltpu.make_async_copy(from_ref.at[rows], to_ref.at[rows], sems.at[len(copies)])
        copy.start()
        copies.append(copy)

    for h in range(2):
        block = recv_ref[pl.ds(32 + h, MEMBERS, stride=ROWS), :]
        fg_ref[:, h * B : (h + 1) * B] = block * (1.0 / math.sqrt(N))
    store(fg_ref, fg_hbm, pl.ds(0, 64))
    for h in range(2):
        rows = slice(h * B, (h + 1) * B)
        for k in range(4):
            cols = pl.ds(pl.multiple_of(pairs[k] * B, B), B)
            og_ref[rows, cols] = (cot_ref[rows, cols].astype(F32) * fetch(0, h, k)).astype(BF)
        store(og_ref, og_hbm, pl.ds(h * B, B))
        for k in range(4):
            cols = pl.ds(pl.multiple_of(pairs[k] * B, B), B)
            back = fetch(16, h, k)
            ig_ref[rows, cols] = (back * signal_ref[rows, cols].astype(F32)).astype(BF)
            sg_ref[rows, cols] = (back * inner_ref[rows, cols].astype(F32)).astype(BF)
        store(ig_ref, ig_hbm, pl.ds(h * B, B))
        store(sg_ref, sg_hbm, pl.ds(h * B, B))
    for copy in copies:
        copy.wait()


def call(kernel, out_shapes, name, scratch=(), cost=(0, 0), ins=None, outs=None):
    return pl.pallas_call(
        kernel,
        out_shape=out_shapes,
        in_specs=pl.no_block_spec if ins is None else ins,
        scratch_shapes=list(scratch),
        name=name,
        out_specs=pl.no_block_spec if outs is None else outs,
        compiler_params=pltpu.CompilerParams(vmem_limit_bytes=VMEM_LIMIT),
        cost_estimate=pl.CostEstimate(flops=cost[0], bytes_accessed=cost[1], transcendentals=0),
    )


def shape(*dims, dtype=F32):
    return jax.ShapeDtypeStruct(dims, dtype)


PAIRS = [[s * 8 + 2 * p + q for q in range(2) for s in SCATTER.tolist()] for p in range(4)]


def exchange(x):
    x = x.reshape(MEMBERS, ROWS * B)
    x = lax.all_to_all(x, ("seq", "chan"), 0, 0, axis_index_groups=PAIRS, tiled=True)
    return x.reshape(MEMBERS * ROWS, B)


def swap(x, distance):
    return lax.ppermute(x, "chan", [(z, z ^ distance) for z in range(8)])


def body(outer_gate, inner_gate, signal, cotangent, filters):
    w1, w2h, w2l, tw, v1 = [jnp.asarray(t) for t in tables()]
    buffer = shape(MEMBERS * ROWS, B)
    two = shape(2, A, B)
    gate = pltpu.VMEM((256, 512), BF)
    send = call(
        prep_kernel, buffer, "prep",
        [gate, gate, gate, gate, pltpu.VMEM((64, 256), F32), pltpu.SemaphoreType.DMA((9,))],
        ins=[pl.BlockSpec(memory_space=pltpu.HBM)] * 5,
    )(*[
        pltpu.with_memory_space_constraint(x, pltpu.HBM)
        for x in (outer_gate, inner_gate, signal, cotangent, filters.T)
    ])
    recv = exchange(send)
    own = call(pick_kernel, two, "pick")(recv)
    f3 = swap(own, 6)
    tables_in = (w1, w2h, w2l, tw, v1)

    def spectra(first):
        return call(
            functools.partial(spectra_kernel, first=first),
            (shape(4, 2 * A, 2 * B), shape(4, 2 * A, 2 * B), shape(4, A, B)),
            "spectra",
            [pltpu.VMEM((4, A, 2 * B), F32)],
            (1_000_000_000, 2_000_000),
        )(recv, *tables_in)

    u1, g1, away = spectra(4)
    came = swap(away, 6)
    u0, g0, near = spectra(0)
    f3, near = lax.optimization_barrier((f3, near))
    far = swap(jnp.stack([own, f3]), 2)
    even = call(conv_even_kernel, buffer, "even", cost=(1_000_000_000, 2_000_000))(
        own, f3, u0, g0, u1, g1, *tables_in
    )
    keep, give = call(mix_kernel, (two, two), "mix")(near, came)
    came = swap(give, 2)
    odd = call(conv_odd_kernel, buffer, "odd", cost=(1_000_000_000, 2_000_000))(
        far, even, u0, g0, u1, g1, *tables_in
    )
    back_send = call(place_kernel, buffer, "place")(keep, came, odd)
    landed = exchange(back_send)
    *grads, fg = call(
        post_kernel,
        (shape(256, 512, dtype=BF), shape(256, 512, dtype=BF), shape(256, 512, dtype=BF), shape(64, 256)),
        "post",
        [gate, gate, gate, pltpu.VMEM((64, 256), F32), pltpu.SemaphoreType.DMA((7,))],
        outs=[pl.BlockSpec(memory_space=pltpu.HBM)] * 4,
    )(landed, inner_gate, signal, cotangent)
    return (*grads, fg.T)


def solution(mesh):
    spec = P("seq", "chan")
    return jax.shard_map(
        body, mesh=mesh, in_specs=(spec,) * 5, out_specs=(spec,) * 4, check_vma=False
    )
```

```python
import functools
import math

import jax
import jax.numpy as jnp
import numpy as np
import ml_dtypes
from jax import lax
from jax.experimental import pallas as pl
from jax.experimental.pallas import tpu as pltpu
from jax.sharding import PartitionSpec as P

BF = jnp.bfloat16
F32 = jnp.float32

N = 8192
A = 64
B = 128
SHARDS = 32
MEMBERS = 64
ROWS = 34
SCATTER = np.random.RandomState(3).permutation(SHARDS)
VMEM_LIMIT = 16 * 1024 * 1024


def two_parts(table):
    high = table.astype(ml_dtypes.bfloat16)
    low = (table - high.astype(np.float64)).astype(ml_dtypes.bfloat16)
    return high, low


def tables():
    order = np.array([2 * s + h for h in range(2) for s in SCATTER])
    k1 = np.arange(A) - 0.25
    angle1 = 2 * np.pi / A * np.outer(k1, order)
    w1 = np.concatenate([np.cos(angle1), -np.sin(angle1)], axis=0)
    high, low = two_parts(w1)
    w1cat = np.concatenate([high, high, low], axis=1)
    v1 = np.concatenate([np.cos(angle1), -np.sin(angle1)], axis=0).T / N
    high, low = two_parts(v1)
    v1cat = np.concatenate([high, high, low], axis=1)
    angle2 = 2 * np.pi / B * np.outer(np.arange(B), np.arange(B))
    c, s = np.cos(angle2), np.sin(angle2)
    w2 = np.block([[c, -s], [s, c]])
    w2h, w2l = two_parts(w2)
    angle = 2 * np.pi / N * np.outer(k1, np.arange(B))
    twiddle = np.stack([np.cos(angle), np.sin(angle)]).astype(np.float32)
    return w1cat, w2h, w2l, twiddle, v1cat


def split(x):
    high = x.astype(BF)
    return high, (x - high.astype(F32)).astype(BF)


def dot(x, y):
    return jnp.dot(x, y, preferred_element_type=F32)


def first_stage(columns, w1, c, s):
    high, low = split(jnp.concatenate(columns, axis=1))
    out = dot(w1, jnp.concatenate([high, low, high], axis=0))
    pairs = []
    for i in range(len(columns)):
        re = out[:A, i * B : (i + 1) * B]
        im = out[A:, i * B : (i + 1) * B]
        pairs.append((re * c + im * s, im * c - re * s))
    return pairs


def second_stage(pairs, high_table, low_table):
    stacked = jnp.concatenate([jnp.concatenate(p, axis=1) for p in pairs], axis=0)
    high, low = split(stacked)
    return dot(high, high_table) + dot(low, high_table) + dot(high, low_table)


def last_stage(blocks, v1, c, s):
    re, im = [], []
    for block in blocks:
        qi, qr = block[:, :B], block[:, B:]
        re.append(qr * c - qi * s)
        im.append(qr * s + qi * c)
    both = jnp.concatenate([jnp.concatenate(re, axis=1), jnp.concatenate(im, axis=1)], axis=0)
    high, low = split(both)
    vh, vl = v1[:, : 2 * A], v1[:, 4 * A :]
    return dot(v1[:, : 4 * A], jnp.concatenate([high, low], axis=0)) + dot(vl, high)


def forward(columns, w1, w2h, w2l, c, s):
    return second_stage(first_stage(columns, w1, c, s), w2h, w2l)


def prep_kernel(outer_hbm, inner_hbm, signal_hbm, cot_hbm, filt_hbm, send_ref,
                outer_ref, inner_ref, signal_ref, cot_ref, filt_ref, sems):
    def load(i, from_ref, to_ref, rows):
        copy = pltpu.make_async_copy(from_ref.at[rows], to_ref.at[rows], sems.at[i])
        copy.start()
        return copy

    halves = [pl.ds(0, B), pl.ds(B, B)]
    arrays = [(inner_hbm, inner_ref), (signal_hbm, signal_ref), (cot_hbm, cot_ref), (outer_hbm, outer_ref)]
    copies = [load(i * 4 + j, *pair, rows) for i, rows in enumerate(halves) for j, pair in enumerate(arrays)]
    last = load(8, filt_hbm, filt_ref, pl.ds(0, 64))

    pairs = partners()

    def place(block, first_row, h, k):
        turned = block.T
        for e in range(2):
            row = first_row + h * 8 + k * 2 + e
            send_ref[pl.ds(row, MEMBERS, stride=ROWS), :] = turned[e * 64 : (e + 1) * 64]

    for h in range(2):
        rows = slice(h * B, (h + 1) * B)
        for copy in copies[h * 4 : h * 4 + 4]:
            copy.wait()
        for k in range(4):
            cols = pl.ds(pl.multiple_of(pairs[k] * B, B), B)
            place(inner_ref[rows, cols].astype(F32) * signal_ref[rows, cols].astype(F32), 0, h, k)
            place(cot_ref[rows, cols].astype(F32) * outer_ref[rows, cols].astype(F32), 16, h, k)
    last.wait()
    for h in range(2):
        send_ref[pl.ds(32 + h, MEMBERS, stride=ROWS), :] = filt_ref[:, h * B : (h + 1) * B]


def partners():
    pair = lax.axis_index("chan") // 2
    beside = pair + 1 - 2 * lax.rem(pair, 2)
    return [pair, beside, lax.rem(pair + 2, 4), lax.rem(beside + 2, 4)]


def gather_rows(ref, q, row, step):
    return jnp.concatenate(
        [ref[pl.ds(q * 32 * ROWS + row + step * h, 32, stride=ROWS), :] for h in range(2)], axis=0
    )


def pick_kernel(recv_ref, out_ref):
    for q in range(2):
        out_ref[q] = gather_rows(recv_ref, q, 32, 1)


def spectra_kernel(recv_ref, w1_ref, w2h_ref, w2l_ref, tw_ref, v1_ref, u_ref, g_ref, fg_ref,
                   prod_ref, *, first, count):
    c, s = tw_ref[0], tw_ref[1]
    for f in range(count):
        columns = [gather_rows(recv_ref, q, first + f + base, 8) for base in (0, 16) for q in range(2)]
        spec = forward(columns, w1_ref[...], w2h_ref[...], w2l_ref[...], c, s)
        u_ref[f] = spec[: 2 * A]
        g_ref[f] = spec[2 * A :]
        ur, ui = spec[: 2 * A, :B], spec[: 2 * A, B:]
        gr, gi = spec[2 * A :, :B], spec[2 * A :, B:]
        pr = gr * ur + gi * ui
        pi = gi * ur - gr * ui
        prod_ref[f] = jnp.concatenate([pi[:A] + pi[A:], pr[:A] + pr[A:]], axis=1)
    high, low = split(prod_ref[...].reshape(count * A, 2 * B))
    mid = dot(high, w2h_ref[...]) + dot(low, w2h_ref[...]) + dot(high, w2l_ref[...])
    out = last_stage([mid[i * A : (i + 1) * A] for i in range(count)], v1_ref[...], c, s)
    for i in range(count):
        fg_ref[i] = out[:, i * B : (i + 1) * B]


def mix_kernel(near_ref, came_ref, give_ref):
    give_ref[...] = near_ref[2:4] + came_ref[...]


def conv_part(ks, filts, u_refs, g_refs, w1, w2h, w2l, tw_ref, v1, out_ref):
    c, s = tw_ref[0], tw_ref[1]
    spec = forward([filt[q] for filt in filts for q in range(2)], w1, w2h, w2l, c, s)
    prods, places = [], []
    for j, k in enumerate(ks):
        for e in range(2):
            f = 2 * k + e
            u_ref, g_ref, at = u_refs[k], g_refs[k], f % (2 if k > 1 else 4)
            h_spec = spec[(2 * j + e) * A : (2 * j + e + 1) * A]
            hr, hi = h_spec[:, :B], h_spec[:, B:]
            for q in range(2):
                ur, ui = u_ref[at, q * A : (q + 1) * A, :B], u_ref[at, q * A : (q + 1) * A, B:]
                prods.append((hr * ui + hi * ur, hr * ur - hi * ui))
                places.append((q, f))
            for q in range(2):
                gr, gi = g_ref[at, q * A : (q + 1) * A, :B], g_ref[at, q * A : (q + 1) * A, B:]
                prods.append((gi * hr - gr * hi, gr * hr + gi * hi))
                places.append((q, 16 + f))
    mid = second_stage(prods, w2h, w2l)
    for n in range(0, 16, 4):
        out = last_stage([mid[i * A : (i + 1) * A] for i in range(n, n + 4)], v1, c, s)
        for i in range(4):
            q, row = places[n + i]
            for h in range(2):
                out_ref[pl.ds(q * 32 * ROWS + row + 8 * h, 32, stride=ROWS), :] = (
                    out[h * 32 : (h + 1) * 32, i * B : (i + 1) * B]
                )


def conv_even_kernel(own_ref, f3_ref, u0_ref, g0_ref, u2_ref, g2_ref, u3_ref, g3_ref, w1_ref, w2h_ref, w2l_ref, tw_ref, v1_ref,
                     out_ref):
    conv_part((0, 3), (own_ref, f3_ref), (u0_ref, u0_ref, u2_ref, u3_ref), (g0_ref, g0_ref, g2_ref, g3_ref), w1_ref[...], w2h_ref[...], w2l_ref[...], tw_ref,
              v1_ref[...], out_ref)


def conv_odd_kernel(far_ref, base_ref, u0_ref, g0_ref, u2_ref, g2_ref, u3_ref, g3_ref, w1_ref, w2h_ref, w2l_ref,
                    tw_ref, v1_ref, out_ref):
    out_ref[...] = base_ref[...]
    conv_part((1, 2), (far_ref.at[0], far_ref.at[1]), (u0_ref, u0_ref, u2_ref, u3_ref), (g0_ref, g0_ref, g2_ref, g3_ref), w1_ref[...], w2h_ref[...],
              w2l_ref[...], tw_ref, v1_ref[...], out_ref)


def place_kernel(near_ref, fg3_ref, came_ref, base_ref, out_ref):
    out_ref[...] = base_ref[...]
    for q in range(2):
        total = near_ref[q] + fg3_ref[q] + came_ref[q]
        for h in range(2):
            out_ref[pl.ds(q * 32 * ROWS + 32 + h, 32, stride=ROWS), :] = total[h * 32 : (h + 1) * 32]


def post_kernel(recv_ref, inner_ref, signal_ref, cot_ref, og_hbm, ig_hbm, sg_hbm, fg_hbm,
                og_ref, ig_ref, sg_ref, fg_ref, sems):
    pairs = partners()

    def fetch(first_row, h, k):
        blocks = [
            recv_ref[pl.ds(first_row + h * 8 + k * 2 + e, MEMBERS, stride=ROWS), :] for e in range(2)
        ]
        return jnp.concatenate(blocks, axis=0).T

    copies = []

    def store(from_ref, to_ref, rows):
        copy = pltpu.make_async_copy(from_ref.at[rows], to_ref.at[rows], sems.at[len(copies)])
        copy.start()
        copies.append(copy)

    for h in range(2):
        block = recv_ref[pl.ds(32 + h, MEMBERS, stride=ROWS), :]
        fg_ref[:, h * B : (h + 1) * B] = block * (1.0 / math.sqrt(N))
    store(fg_ref, fg_hbm, pl.ds(0, 64))
    for h in range(2):
        rows = slice(h * B, (h + 1) * B)
        for k in range(4):
            cols = pl.ds(pl.multiple_of(pairs[k] * B, B), B)
            og_ref[rows, cols] = (cot_ref[rows, cols].astype(F32) * fetch(0, h, k)).astype(BF)
        store(og_ref, og_hbm, pl.ds(h * B, B))
        for k in range(4):
            cols = pl.ds(pl.multiple_of(pairs[k] * B, B), B)
            back = fetch(16, h, k)
            ig_ref[rows, cols] = (back * signal_ref[rows, cols].astype(F32)).astype(BF)
            sg_ref[rows, cols] = (back * inner_ref[rows, cols].astype(F32)).astype(BF)
        store(ig_ref, ig_hbm, pl.ds(h * B, B))
        store(sg_ref, sg_hbm, pl.ds(h * B, B))
    for copy in copies:
        copy.wait()


def call(kernel, out_shapes, name, scratch=(), cost=(1000, 1000), ins=None, outs=None):
    return pl.pallas_call(
        kernel,
        out_shape=out_shapes,
        in_specs=pl.no_block_spec if ins is None else ins,
        scratch_shapes=list(scratch),
        name=name,
        out_specs=pl.no_block_spec if outs is None else outs,
        compiler_params=pltpu.CompilerParams(vmem_limit_bytes=VMEM_LIMIT),
        cost_estimate=pl.CostEstimate(flops=cost[0], bytes_accessed=cost[1], transcendentals=0),
    )


def shape(*dims, dtype=F32):
    return jax.ShapeDtypeStruct(dims, dtype)


PAIRS = [[s * 8 + 2 * p + q for q in range(2) for s in SCATTER.tolist()] for p in range(4)]


def exchange(x):
    x = x.reshape(MEMBERS, ROWS * B)
    x = lax.all_to_all(x, ("seq", "chan"), 0, 0, axis_index_groups=PAIRS, tiled=True)
    return x.reshape(MEMBERS * ROWS, B)


def swap(x, distance):
    return lax.ppermute(x, "chan", [(z, z ^ distance) for z in range(8)])


def body(outer_gate, inner_gate, signal, cotangent, filters):
    w1, w2h, w2l, tw, v1 = [jnp.asarray(t) for t in tables()]
    buffer = shape(MEMBERS * ROWS, B)
    two = shape(2, A, B)
    gate = pltpu.VMEM((256, 512), BF)
    send = call(
        prep_kernel, buffer, "prep",
        [gate, gate, gate, gate, pltpu.VMEM((64, 256), F32), pltpu.SemaphoreType.DMA((9,))],
        ins=[pl.BlockSpec(memory_space=pltpu.HBM)] * 5,
    )(*[
        pltpu.with_memory_space_constraint(x, pltpu.HBM)
        for x in (outer_gate, inner_gate, signal, cotangent, filters.T)
    ])
    recv = exchange(send)
    own = call(pick_kernel, two, "pick")(recv)
    f3 = swap(own, 6)
    tables_in = (w1, w2h, w2l, tw, v1)

    def spectra(recv, first, count):
        return call(
            functools.partial(spectra_kernel, first=first, count=count),
            (shape(count, 2 * A, 2 * B), shape(count, 2 * A, 2 * B), shape(count, A, B)),
            "spectra",
            [pltpu.VMEM((count, A, 2 * B), F32)],
            (1000, 1000),
        )(recv, *tables_in)

    u2, g2, fg2 = spectra(recv, 4, 2)
    relay = swap(fg2, 6)
    recv, fg2 = lax.optimization_barrier((recv, fg2))
    u3, g3, fg3 = spectra(recv, 6, 2)
    fg3 = swap(fg3, 6)
    recv, g3 = lax.optimization_barrier((recv, g3))
    u0, g0, near = spectra(recv, 0, 4)
    f3, near = lax.optimization_barrier((f3, near))
    far = swap(jnp.stack([own, f3]), 2)
    even = call(conv_even_kernel, buffer, "even", cost=(1000, 1000))(
        own, f3, u0, g0, u2, g2, u3, g3, *tables_in
    )
    came = swap(call(mix_kernel, two, "mix")(near, relay), 2)
    odd = call(conv_odd_kernel, buffer, "odd", cost=(1000, 1000))(
        far, even, u0, g0, u2, g2, u3, g3, *tables_in
    )
    back_send = call(place_kernel, buffer, "place")(near, fg3, came, odd)
    landed = exchange(back_send)
    *grads, fg = call(
        post_kernel,
        (shape(256, 512, dtype=BF), shape(256, 512, dtype=BF), shape(256, 512, dtype=BF), shape(64, 256)),
        "post",
        [gate, gate, gate, pltpu.VMEM((64, 256), F32), pltpu.SemaphoreType.DMA((7,))],
        outs=[pl.BlockSpec(memory_space=pltpu.HBM)] * 4,
    )(landed, inner_gate, signal, cotangent)
    return (*grads, fg.T)


def solution(mesh):
    spec = P("seq", "chan")
    return jax.shard_map(
        body, mesh=mesh, in_specs=(spec,) * 5, out_specs=(spec,) * 4, check_vma=False
    )
```

```python
import functools
import math

import jax
import jax.numpy as jnp
import numpy as np
import ml_dtypes
from jax import lax
from jax.experimental import pallas as pl
from jax.experimental.pallas import tpu as pltpu
from jax.sharding import PartitionSpec as P

BF = jnp.bfloat16
F32 = jnp.float32

N = 8192
A = 64
B = 128
SHARDS = 32
MEMBERS = 64
ROWS = 34
SCATTER = np.random.RandomState(3).permutation(SHARDS)
VMEM_LIMIT = 16 * 1024 * 1024


def two_parts(table):
    high = table.astype(ml_dtypes.bfloat16)
    low = (table - high.astype(np.float64)).astype(ml_dtypes.bfloat16)
    return high, low


def tables():
    order = np.array([2 * s + h for h in range(2) for s in SCATTER])
    k1 = np.arange(A) - 0.25
    angle1 = 2 * np.pi / A * np.outer(k1, order)
    w1 = np.concatenate([np.cos(angle1), -np.sin(angle1)], axis=0)
    high, low = two_parts(w1)
    w1cat = np.concatenate([high, high, low], axis=1)
    v1 = np.concatenate([np.cos(angle1), -np.sin(angle1)], axis=0).T / N
    high, low = two_parts(v1)
    v1cat = np.concatenate([high, high, low], axis=1)
    angle2 = 2 * np.pi / B * np.outer(np.arange(B), np.arange(B))
    c, s = np.cos(angle2), np.sin(angle2)
    w2 = np.block([[c, -s], [s, c]])
    w2h, w2l = two_parts(w2)
    angle = 2 * np.pi / N * np.outer(k1, np.arange(B))
    twiddle = np.stack([np.cos(angle), np.sin(angle)]).astype(np.float32)
    return w1cat, w2h, w2l, twiddle, v1cat


def split(x):
    high = x.astype(BF)
    return high, (x - high.astype(F32)).astype(BF)


def dot(x, y):
    return jnp.dot(x, y, preferred_element_type=F32)


def first_stage(columns, w1, c, s):
    high, low = split(jnp.concatenate(columns, axis=1))
    out = dot(w1, jnp.concatenate([high, low, high], axis=0))
    pairs = []
    for i in range(len(columns)):
        re = out[:A, i * B : (i + 1) * B]
        im = out[A:, i * B : (i + 1) * B]
        pairs.append((re * c + im * s, im * c - re * s))
    return pairs


def second_stage(pairs, high_table, low_table):
    stacked = jnp.concatenate([jnp.concatenate(p, axis=1) for p in pairs], axis=0)
    high, low = split(stacked)
    return dot(high, high_table) + dot(low, high_table) + dot(high, low_table)


def last_stage(blocks, v1, c, s):
    re, im = [], []
    for block in blocks:
        qi, qr = block[:, :B], block[:, B:]
        re.append(qr * c - qi * s)
        im.append(qr * s + qi * c)
    both = jnp.concatenate([jnp.concatenate(re, axis=1), jnp.concatenate(im, axis=1)], axis=0)
    high, low = split(both)
    vh, vl = v1[:, : 2 * A], v1[:, 4 * A :]
    return dot(v1[:, : 4 * A], jnp.concatenate([high, low], axis=0)) + dot(vl, high)


def forward(columns, w1, w2h, w2l, c, s):
    return second_stage(first_stage(columns, w1, c, s), w2h, w2l)


def prep_kernel(outer_hbm, inner_hbm, signal_hbm, cot_hbm, filt_hbm, send_ref,
                outer_ref, inner_ref, signal_ref, cot_ref, filt_ref, sems):
    def load(i, from_ref, to_ref, rows):
        copy = pltpu.make_async_copy(from_ref.at[rows], to_ref.at[rows], sems.at[i])
        copy.start()
        return copy

    halves = [pl.ds(0, B), pl.ds(B, B)]
    arrays = [(inner_hbm, inner_ref), (signal_hbm, signal_ref), (cot_hbm, cot_ref), (outer_hbm, outer_ref)]
    copies = [load(i * 4 + j, *pair, rows) for i, rows in enumerate(halves) for j, pair in enumerate(arrays)]
    last = load(8, filt_hbm, filt_ref, pl.ds(0, 64))

    pairs = partners()

    def place(block, first_row, h, k):
        turned = block.T
        for e in range(2):
            row = first_row + h * 8 + k * 2 + e
            send_ref[pl.ds(row, MEMBERS, stride=ROWS), :] = turned[e * 64 : (e + 1) * 64]

    for h in range(2):
        rows = slice(h * B, (h + 1) * B)
        for copy in copies[h * 4 : h * 4 + 4]:
            copy.wait()
        for k in range(4):
            cols = pl.ds(pl.multiple_of(pairs[k] * B, B), B)
            place(inner_ref[rows, cols].astype(F32) * signal_ref[rows, cols].astype(F32), 0, h, k)
            place(cot_ref[rows, cols].astype(F32) * outer_ref[rows, cols].astype(F32), 16, h, k)
    last.wait()
    for h in range(2):
        send_ref[pl.ds(32 + h, MEMBERS, stride=ROWS), :] = filt_ref[:, h * B : (h + 1) * B]


def partners():
    pair = lax.axis_index("chan") // 2
    beside = pair + 1 - 2 * lax.rem(pair, 2)
    return [pair, beside, lax.rem(pair + 2, 4), lax.rem(beside + 2, 4)]


def gather_rows(ref, q, row, step):
    return jnp.concatenate(
        [ref[pl.ds(q * 32 * ROWS + row + step * h, 32, stride=ROWS), :] for h in range(2)], axis=0
    )


def pick_kernel(recv_ref, w1_ref, w2h_ref, w2l_ref, tw_ref, v1_ref, out_ref):
    for q in range(2):
        out_ref[q] = gather_rows(recv_ref, q, 32, 1)


def spectra_kernel(recv_ref, w1_ref, w2h_ref, w2l_ref, tw_ref, v1_ref, u_ref, g_ref, *rest,
                   channels):
    c, s = tw_ref[0], tw_ref[1]
    count = len(channels)
    *fg_refs, prod_ref = rest
    fg_places = [(ref, i) for ref in fg_refs for i in range(ref.shape[0])]
    for f, channel in enumerate(channels):
        columns = [gather_rows(recv_ref, q, channel + base, 8) for base in (0, 16) for q in range(2)]
        spec = forward(columns, w1_ref[...], w2h_ref[...], w2l_ref[...], c, s)
        u_ref[f] = spec[: 2 * A]
        g_ref[f] = spec[2 * A :]
        ur, ui = spec[: 2 * A, :B], spec[: 2 * A, B:]
        gr, gi = spec[2 * A :, :B], spec[2 * A :, B:]
        pr = gr * ur + gi * ui
        pi = gi * ur - gr * ui
        prod_ref[f] = jnp.concatenate([pi[:A] + pi[A:], pr[:A] + pr[A:]], axis=1)
    high, low = split(prod_ref[...].reshape(count * A, 2 * B))
    mid = dot(high, w2h_ref[...]) + dot(low, w2h_ref[...]) + dot(high, w2l_ref[...])
    out = last_stage([mid[i * A : (i + 1) * A] for i in range(count)], v1_ref[...], c, s)
    for i in range(count):
        fg_ref, place = fg_places[i]
        fg_ref[place] = out[:, i * B : (i + 1) * B]


def mix_kernel(near_ref, came_ref, give_ref):
    give_ref[...] = near_ref[2:4] + came_ref[...]


def conv_part(ks, filts, u_ref, g_ref, starts, w1, w2h, w2l, tw_ref, v1, out_ref):
    c, s = tw_ref[0], tw_ref[1]
    spec = forward([filt[q] for filt in filts for q in range(2)], w1, w2h, w2l, c, s)
    prods, places = [], []
    for j, k in enumerate(ks):
        for e in range(2):
            f = 2 * k + e
            at = starts[j] + e
            h_spec = spec[(2 * j + e) * A : (2 * j + e + 1) * A]
            hr, hi = h_spec[:, :B], h_spec[:, B:]
            for q in range(2):
                ur, ui = u_ref[at, q * A : (q + 1) * A, :B], u_ref[at, q * A : (q + 1) * A, B:]
                prods.append((hr * ui + hi * ur, hr * ur - hi * ui))
                places.append((q, f))
            for q in range(2):
                gr, gi = g_ref[at, q * A : (q + 1) * A, :B], g_ref[at, q * A : (q + 1) * A, B:]
                prods.append((gi * hr - gr * hi, gr * hr + gi * hi))
                places.append((q, 16 + f))
    mid = second_stage(prods, w2h, w2l)
    for n in range(0, len(prods), 4):
        out = last_stage([mid[i * A : (i + 1) * A] for i in range(n, n + 4)], v1, c, s)
        for i in range(4):
            q, row = places[n + i]
            for h in range(2):
                out_ref[pl.ds(q * 32 * ROWS + row + 8 * h, 32, stride=ROWS), :] = (
                    out[h * 32 : (h + 1) * 32, i * B : (i + 1) * B]
                )


def conv_three_kernel(own_ref, fb_ref, fa_ref, u_ref, g_ref, w1_ref, w2h_ref, w2l_ref, tw_ref, v1_ref,
                      out_ref):
    conv_part((0, 1, 3), (own_ref, fb_ref, fa_ref), u_ref, g_ref, (2, 4, 0), w1_ref[...], w2h_ref[...],
              w2l_ref[...], tw_ref, v1_ref[...], out_ref)


def conv_last_kernel(far_ref, base_ref, u_ref, g_ref, w1_ref, w2h_ref, w2l_ref, tw_ref, v1_ref, out_ref):
    out_ref[...] = base_ref[...]
    conv_part((2,), (far_ref,), u_ref, g_ref, (0,), w1_ref[...], w2h_ref[...], w2l_ref[...], tw_ref,
              v1_ref[...], out_ref)


def place_kernel(near_ref, direct_ref, came_ref, base_ref, out_ref):
    out_ref[...] = base_ref[...]
    for q in range(2):
        total = near_ref[q] + direct_ref[q] + came_ref[q]
        for h in range(2):
            out_ref[pl.ds(q * 32 * ROWS + 32 + h, 32, stride=ROWS), :] = total[h * 32 : (h + 1) * 32]


def post_kernel(recv_ref, inner_ref, signal_ref, cot_ref, og_hbm, ig_hbm, sg_hbm, fg_hbm,
                og_ref, ig_ref, sg_ref, fg_ref, sems):
    pairs = partners()

    def fetch(first_row, h, k):
        blocks = [
            recv_ref[pl.ds(first_row + h * 8 + k * 2 + e, MEMBERS, stride=ROWS), :] for e in range(2)
        ]
        return jnp.concatenate(blocks, axis=0).T

    copies = []

    def store(from_ref, to_ref, rows):
        copy = pltpu.make_async_copy(from_ref.at[rows], to_ref.at[rows], sems.at[len(copies)])
        copy.start()
        copies.append(copy)

    for h in range(2):
        block = recv_ref[pl.ds(32 + h, MEMBERS, stride=ROWS), :]
        fg_ref[:, h * B : (h + 1) * B] = block * (1.0 / math.sqrt(N))
    store(fg_ref, fg_hbm, pl.ds(0, 64))
    for h in range(2):
        rows = slice(h * B, (h + 1) * B)
        for k in range(4):
            cols = pl.ds(pl.multiple_of(pairs[k] * B, B), B)
            og_ref[rows, cols] = (cot_ref[rows, cols].astype(F32) * fetch(0, h, k)).astype(BF)
        store(og_ref, og_hbm, pl.ds(h * B, B))
        for k in range(4):
            cols = pl.ds(pl.multiple_of(pairs[k] * B, B), B)
            back = fetch(16, h, k)
            ig_ref[rows, cols] = (back * signal_ref[rows, cols].astype(F32)).astype(BF)
            sg_ref[rows, cols] = (back * inner_ref[rows, cols].astype(F32)).astype(BF)
        store(ig_ref, ig_hbm, pl.ds(h * B, B))
        store(sg_ref, sg_hbm, pl.ds(h * B, B))
    for copy in copies:
        copy.wait()


def call(kernel, out_shapes, name, scratch=(), cost=(1000, 1000), ins=None, outs=None):
    return pl.pallas_call(
        kernel,
        out_shape=out_shapes,
        in_specs=pl.no_block_spec if ins is None else ins,
        scratch_shapes=list(scratch),
        name=name,
        out_specs=pl.no_block_spec if outs is None else outs,
        compiler_params=pltpu.CompilerParams(vmem_limit_bytes=VMEM_LIMIT),
        cost_estimate=pl.CostEstimate(flops=cost[0], bytes_accessed=cost[1], transcendentals=0),
    )


def shape(*dims, dtype=F32):
    return jax.ShapeDtypeStruct(dims, dtype)


PAIRS = [[s * 8 + 2 * p + q for q in range(2) for s in SCATTER.tolist()] for p in range(4)]


def exchange(x):
    x = x.reshape(MEMBERS, ROWS * B)
    x = lax.all_to_all(x, ("seq", "chan"), 0, 0, axis_index_groups=PAIRS, tiled=True)
    return x.reshape(MEMBERS * ROWS, B)


def swap(x, distance):
    return lax.ppermute(x, "chan", [(z, z ^ distance) for z in range(8)])


def body(outer_gate, inner_gate, signal, cotangent, filters):
    w1, w2h, w2l, tw, v1 = [jnp.asarray(t) for t in tables()]
    buffer = shape(MEMBERS * ROWS, B)
    two = shape(2, A, B)
    gate = pltpu.VMEM((256, 512), BF)
    send = call(
        prep_kernel, buffer, "prep",
        [gate, gate, gate, gate, pltpu.VMEM((64, 256), F32), pltpu.SemaphoreType.DMA((9,))],
        ins=[pl.BlockSpec(memory_space=pltpu.HBM)] * 5,
    )(*[
        pltpu.with_memory_space_constraint(x, pltpu.HBM)
        for x in (outer_gate, inner_gate, signal, cotangent, filters.T)
    ])
    recv = exchange(send)
    tables_in = (w1, w2h, w2l, tw, v1)
    own = call(pick_kernel, two, "pick")(recv, *tables_in)
    fa, fb = swap(own, 6), swap(own, 2)
    def spectra(recv, ks, sizes):
        channels = [2 * k + e for k in ks for e in range(2)]
        count = len(channels)
        return call(
            functools.partial(spectra_kernel, channels=channels),
            (shape(count, 2 * A, 2 * B), shape(count, 2 * A, 2 * B))
            + tuple(shape(size, A, B) for size in sizes),
            "spectra",
            [pltpu.VMEM((count, A, 2 * B), F32)],
            (1000, 1000),
        )(recv, *tables_in)

    ur, gr, relay = spectra(recv, (2,), (2,))
    recv, relay = lax.optimization_barrier((recv, relay))
    relay = swap(relay, 6)
    un, gn, direct, near = spectra(recv, (3, 0, 1), (2, 4))
    fb, near = lax.optimization_barrier((fb, near))
    far = swap(fb, 6)
    direct = swap(direct, 6)
    three = call(conv_three_kernel, buffer, "three", cost=(1000, 1000))(
        own, fb, fa, un, gn, *tables_in
    )
    came = swap(call(mix_kernel, two, "mix")(near, relay), 2)
    last = call(conv_last_kernel, buffer, "last", cost=(1000, 1000))(far, three, ur, gr, *tables_in)
    back_send = call(place_kernel, buffer, "place")(near, direct, came, last)
    landed = exchange(back_send)
    *grads, fg = call(
        post_kernel,
        (shape(256, 512, dtype=BF), shape(256, 512, dtype=BF), shape(256, 512, dtype=BF), shape(64, 256)),
        "post",
        [gate, gate, gate, pltpu.VMEM((64, 256), F32), pltpu.SemaphoreType.DMA((7,))],
        outs=[pl.BlockSpec(memory_space=pltpu.HBM)] * 4,
    )(landed, inner_gate, signal, cotangent)
    return (*grads, fg.T)


def solution(mesh):
    spec = P("seq", "chan")
    return jax.shard_map(
        body, mesh=mesh, in_specs=(spec,) * 5, out_specs=(spec,) * 4, check_vma=False
    )
```

```python
import functools
import math

import jax
import jax.numpy as jnp
import numpy as np
import ml_dtypes
from jax import lax
from jax.experimental import pallas as pl
from jax.experimental.pallas import tpu as pltpu
from jax.sharding import PartitionSpec as P

BF = jnp.bfloat16
F32 = jnp.float32

N = 8192
A = 64
B = 128
SHARDS = 32
MEMBERS = 64
ROWS = 34
SCATTER = np.random.RandomState(10).permutation(SHARDS)
VMEM_LIMIT = 16 * 1024 * 1024


def two_parts(table):
    high = table.astype(ml_dtypes.bfloat16)
    low = (table - high.astype(np.float64)).astype(ml_dtypes.bfloat16)
    return high, low


def tables():
    order = np.array([2 * s + h for h in range(2) for s in SCATTER])
    k1 = np.arange(A) - 0.25
    angle1 = 2 * np.pi / A * np.outer(k1, order)
    w1 = np.concatenate([np.cos(angle1), -np.sin(angle1)], axis=0)
    high, low = two_parts(w1)
    w1cat = np.concatenate([high, high, low], axis=1)
    v1 = np.concatenate([np.cos(angle1), -np.sin(angle1)], axis=0).T / N
    high, low = two_parts(v1)
    v1cat = np.concatenate([high, high, low], axis=1)
    angle2 = 2 * np.pi / B * np.outer(np.arange(B), np.arange(B))
    c, s = np.cos(angle2), np.sin(angle2)
    w2 = np.block([[c, -s], [s, c]])
    w2h, w2l = two_parts(w2)
    angle = 2 * np.pi / N * np.outer(k1, np.arange(B))
    twiddle = np.stack([np.cos(angle), np.sin(angle)]).astype(np.float32)
    return w1cat, w2h, w2l, twiddle, v1cat


def split(x):
    high = x.astype(BF)
    return high, (x - high.astype(F32)).astype(BF)


def dot(x, y):
    return jnp.dot(x, y, preferred_element_type=F32)


def first_stage(columns, w1, c, s):
    high, low = split(jnp.concatenate(columns, axis=1))
    out = dot(w1, jnp.concatenate([high, low, high], axis=0))
    pairs = []
    for i in range(len(columns)):
        re = out[:A, i * B : (i + 1) * B]
        im = out[A:, i * B : (i + 1) * B]
        pairs.append((re * c + im * s, im * c - re * s))
    return pairs


def second_stage(pairs, high_table, low_table):
    stacked = jnp.concatenate([jnp.concatenate(p, axis=1) for p in pairs], axis=0)
    high, low = split(stacked)
    return dot(high, high_table) + dot(low, high_table) + dot(high, low_table)


def last_stage(blocks, v1, c, s):
    re, im = [], []
    for block in blocks:
        qi, qr = block[:, :B], block[:, B:]
        re.append(qr * c - qi * s)
        im.append(qr * s + qi * c)
    both = jnp.concatenate([jnp.concatenate(re, axis=1), jnp.concatenate(im, axis=1)], axis=0)
    high, low = split(both)
    vh, vl = v1[:, : 2 * A], v1[:, 4 * A :]
    return dot(v1[:, : 4 * A], jnp.concatenate([high, low], axis=0)) + dot(vl, high)


def forward(columns, w1, w2h, w2l, c, s):
    return second_stage(first_stage(columns, w1, c, s), w2h, w2l)


def prep_kernel(outer_hbm, inner_hbm, signal_hbm, cot_hbm, filt_hbm, send_ref,
                outer_ref, inner_ref, signal_ref, cot_ref, filt_ref, sems):
    def load(i, from_ref, to_ref, rows):
        copy = pltpu.make_async_copy(from_ref.at[rows], to_ref.at[rows], sems.at[i])
        copy.start()
        return copy

    halves = [pl.ds(0, B), pl.ds(B, B)]
    arrays = [(inner_hbm, inner_ref), (signal_hbm, signal_ref), (cot_hbm, cot_ref), (outer_hbm, outer_ref)]
    copies = [load(i * 4 + j, *pair, rows) for i, rows in enumerate(halves) for j, pair in enumerate(arrays)]
    last = load(8, filt_hbm, filt_ref, pl.ds(0, 64))

    pairs = partners()

    def place(block, first_row, h, k):
        turned = block.T
        for e in range(2):
            row = first_row + h * 8 + k * 2 + e
            send_ref[pl.ds(row, MEMBERS, stride=ROWS), :] = turned[e * 64 : (e + 1) * 64]

    for h in range(2):
        rows = slice(h * B, (h + 1) * B)
        for copy in copies[h * 4 : h * 4 + 4]:
            copy.wait()
        for k in range(4):
            cols = pl.ds(pl.multiple_of(pairs[k] * B, B), B)
            place(inner_ref[rows, cols].astype(F32) * signal_ref[rows, cols].astype(F32), 0, h, k)
            place(cot_ref[rows, cols].astype(F32) * outer_ref[rows, cols].astype(F32), 16, h, k)
    last.wait()
    for h in range(2):
        send_ref[pl.ds(32 + h, MEMBERS, stride=ROWS), :] = filt_ref[:, h * B : (h + 1) * B]


def partners():
    pair = lax.axis_index("chan") // 2
    beside = pair + 1 - 2 * lax.rem(pair, 2)
    return [pair, beside, lax.rem(pair + 2, 4), lax.rem(beside + 2, 4)]


def gather_rows(ref, q, row, step):
    return jnp.concatenate(
        [ref[pl.ds(q * 32 * ROWS + row + step * h, 32, stride=ROWS), :] for h in range(2)], axis=0
    )


def pick_kernel(recv_ref, w1_ref, w2h_ref, w2l_ref, tw_ref, v1_ref, out_ref):
    for q in range(2):
        out_ref[q] = gather_rows(recv_ref, q, 32, 1)


def spectra_kernel(recv_ref, w1_ref, w2h_ref, w2l_ref, tw_ref, v1_ref, u_ref, g_ref, *rest,
                   channels):
    c, s = tw_ref[0], tw_ref[1]
    count = len(channels)
    *fg_refs, prod_ref = rest
    fg_places = [(ref, i) for ref in fg_refs for i in range(ref.shape[0])]
    for f, channel in enumerate(channels):
        columns = [gather_rows(recv_ref, q, channel + base, 8) for base in (0, 16) for q in range(2)]
        spec = forward(columns, w1_ref[...], w2h_ref[...], w2l_ref[...], c, s)
        u_ref[f] = spec[: 2 * A]
        g_ref[f] = spec[2 * A :]
        ur, ui = spec[: 2 * A, :B], spec[: 2 * A, B:]
        gr, gi = spec[2 * A :, :B], spec[2 * A :, B:]
        pr = gr * ur + gi * ui
        pi = gi * ur - gr * ui
        prod_ref[f] = jnp.concatenate([pi[:A] + pi[A:], pr[:A] + pr[A:]], axis=1)
    high, low = split(prod_ref[...].reshape(count * A, 2 * B))
    mid = dot(high, w2h_ref[...]) + dot(low, w2h_ref[...]) + dot(high, w2l_ref[...])
    out = last_stage([mid[i * A : (i + 1) * A] for i in range(count)], v1_ref[...], c, s)
    for i in range(count):
        fg_ref, place = fg_places[i]
        fg_ref[place] = out[:, i * B : (i + 1) * B]


def mix_kernel(near_ref, came_ref, give_ref):
    give_ref[...] = near_ref[2:4] + came_ref[...]


def conv_part(ks, filts, u_ref, g_ref, starts, w1, w2h, w2l, tw_ref, v1, out_ref):
    c, s = tw_ref[0], tw_ref[1]
    spec = forward([filt[q] for filt in filts for q in range(2)], w1, w2h, w2l, c, s)
    prods, places = [], []
    for j, k in enumerate(ks):
        for e in range(2):
            f = 2 * k + e
            at = starts[j] + e
            h_spec = spec[(2 * j + e) * A : (2 * j + e + 1) * A]
            hr, hi = h_spec[:, :B], h_spec[:, B:]
            for q in range(2):
                ur, ui = u_ref[at, q * A : (q + 1) * A, :B], u_ref[at, q * A : (q + 1) * A, B:]
                prods.append((hr * ui + hi * ur, hr * ur - hi * ui))
                places.append((q, f))
            for q in range(2):
                gr, gi = g_ref[at, q * A : (q + 1) * A, :B], g_ref[at, q * A : (q + 1) * A, B:]
                prods.append((gi * hr - gr * hi, gr * hr + gi * hi))
                places.append((q, 16 + f))
    mid = second_stage(prods, w2h, w2l)
    for n in range(0, len(prods), 4):
        out = last_stage([mid[i * A : (i + 1) * A] for i in range(n, n + 4)], v1, c, s)
        for i in range(4):
            q, row = places[n + i]
            for h in range(2):
                out_ref[pl.ds(q * 32 * ROWS + row + 8 * h, 32, stride=ROWS), :] = (
                    out[h * 32 : (h + 1) * 32, i * B : (i + 1) * B]
                )


def conv_three_kernel(own_ref, fb_ref, fa_ref, u_ref, g_ref, w1_ref, w2h_ref, w2l_ref, tw_ref, v1_ref,
                      out_ref):
    conv_part((0, 1, 3), (own_ref, fb_ref, fa_ref), u_ref, g_ref, (2, 4, 0), w1_ref[...], w2h_ref[...],
              w2l_ref[...], tw_ref, v1_ref[...], out_ref)


def conv_last_kernel(far_ref, base_ref, u_ref, g_ref, w1_ref, w2h_ref, w2l_ref, tw_ref, v1_ref, out_ref):
    out_ref[...] = base_ref[...]
    conv_part((2,), (far_ref,), u_ref, g_ref, (0,), w1_ref[...], w2h_ref[...], w2l_ref[...], tw_ref,
              v1_ref[...], out_ref)


def place_kernel(near_ref, direct_ref, came_ref, base_ref, out_ref):
    out_ref[...] = base_ref[...]
    for q in range(2):
        total = near_ref[q] + direct_ref[q] + came_ref[q]
        for h in range(2):
            out_ref[pl.ds(q * 32 * ROWS + 32 + h, 32, stride=ROWS), :] = total[h * 32 : (h + 1) * 32]


def post_kernel(recv_ref, inner_ref, signal_ref, cot_ref, og_hbm, ig_hbm, sg_hbm, fg_hbm,
                og_ref, ig_ref, sg_ref, fg_ref, sems):
    pairs = partners()

    def fetch(first_row, h, k):
        blocks = [
            recv_ref[pl.ds(first_row + h * 8 + k * 2 + e, MEMBERS, stride=ROWS), :] for e in range(2)
        ]
        return jnp.concatenate(blocks, axis=0).T

    copies = []

    def store(from_ref, to_ref, rows):
        copy = pltpu.make_async_copy(from_ref.at[rows], to_ref.at[rows], sems.at[len(copies)])
        copy.start()
        copies.append(copy)

    for h in range(2):
        block = recv_ref[pl.ds(32 + h, MEMBERS, stride=ROWS), :]
        fg_ref[:, h * B : (h + 1) * B] = block * (1.0 / math.sqrt(N))
    store(fg_ref, fg_hbm, pl.ds(0, 64))
    for h in range(2):
        rows = slice(h * B, (h + 1) * B)
        for k in range(4):
            cols = pl.ds(pl.multiple_of(pairs[k] * B, B), B)
            og_ref[rows, cols] = (cot_ref[rows, cols].astype(F32) * fetch(0, h, k)).astype(BF)
        store(og_ref, og_hbm, pl.ds(h * B, B))
        for k in range(4):
            cols = pl.ds(pl.multiple_of(pairs[k] * B, B), B)
            back = fetch(16, h, k)
            ig_ref[rows, cols] = (back * signal_ref[rows, cols].astype(F32)).astype(BF)
            sg_ref[rows, cols] = (back * inner_ref[rows, cols].astype(F32)).astype(BF)
        store(ig_ref, ig_hbm, pl.ds(h * B, B))
        store(sg_ref, sg_hbm, pl.ds(h * B, B))
    for copy in copies:
        copy.wait()


def call(kernel, out_shapes, name, scratch=(), cost=(1000, 1000), ins=None, outs=None):
    return pl.pallas_call(
        kernel,
        out_shape=out_shapes,
        in_specs=pl.no_block_spec if ins is None else ins,
        scratch_shapes=list(scratch),
        name=name,
        out_specs=pl.no_block_spec if outs is None else outs,
        compiler_params=pltpu.CompilerParams(vmem_limit_bytes=VMEM_LIMIT),
        cost_estimate=pl.CostEstimate(flops=cost[0], bytes_accessed=cost[1], transcendentals=0),
    )


def shape(*dims, dtype=F32):
    return jax.ShapeDtypeStruct(dims, dtype)


PAIRS = [[s * 8 + 2 * p + q for q in range(2) for s in SCATTER.tolist()] for p in range(4)]


def exchange(x):
    x = x.reshape(MEMBERS, ROWS * B)
    x = lax.all_to_all(x, ("seq", "chan"), 0, 0, axis_index_groups=PAIRS, tiled=True)
    return x.reshape(MEMBERS * ROWS, B)


def swap(x, distance):
    return lax.ppermute(x, "chan", [(z, z ^ distance) for z in range(8)])


def body(outer_gate, inner_gate, signal, cotangent, filters):
    w1, w2h, w2l, tw, v1 = [jnp.asarray(t) for t in tables()]
    buffer = shape(MEMBERS * ROWS, B)
    two = shape(2, A, B)
    gate = pltpu.VMEM((256, 512), BF)
    send = call(
        prep_kernel, buffer, "prep",
        [gate, gate, gate, gate, pltpu.VMEM((64, 256), F32), pltpu.SemaphoreType.DMA((9,))],
        ins=[pl.BlockSpec(memory_space=pltpu.HBM)] * 5,
    )(*[
        pltpu.with_memory_space_constraint(x, pltpu.HBM)
        for x in (outer_gate, inner_gate, signal, cotangent, filters.T)
    ])
    recv = exchange(send)
    tables_in = (w1, w2h, w2l, tw, v1)
    own = call(pick_kernel, two, "pick")(recv, *tables_in)
    fa, fb = swap(own, 6), swap(own, 2)
    def spectra(recv, ks, sizes):
        channels = [2 * k + e for k in ks for e in range(2)]
        count = len(channels)
        return call(
            functools.partial(spectra_kernel, channels=channels),
            (shape(count, 2 * A, 2 * B), shape(count, 2 * A, 2 * B))
            + tuple(shape(size, A, B) for size in sizes),
            "spectra",
            [pltpu.VMEM((count, A, 2 * B), F32)],
            (1000, 1000),
        )(recv, *tables_in)

    ur, gr, relay = spectra(recv, (2,), (2,))
    recv, relay = lax.optimization_barrier((recv, relay))
    relay = swap(relay, 6)
    un, gn, direct, near = spectra(recv, (3, 0, 1), (2, 4))
    fb, near = lax.optimization_barrier((fb, near))
    far = swap(fb, 6)
    direct = swap(direct, 6)
    three = call(conv_three_kernel, buffer, "three", cost=(1000, 1000))(
        own, fb, fa, un, gn, *tables_in
    )
    came = swap(call(mix_kernel, two, "mix")(near, relay), 2)
    last = call(conv_last_kernel, buffer, "last", cost=(1000, 1000))(far, three, ur, gr, *tables_in)
    back_send = call(place_kernel, buffer, "place")(near, direct, came, last)
    landed = exchange(back_send)
    *grads, fg = call(
        post_kernel,
        (shape(256, 512, dtype=BF), shape(256, 512, dtype=BF), shape(256, 512, dtype=BF), shape(64, 256)),
        "post",
        [gate, gate, gate, pltpu.VMEM((64, 256), F32), pltpu.SemaphoreType.DMA((7,))],
        outs=[pl.BlockSpec(memory_space=pltpu.HBM)] * 4,
    )(landed, inner_gate, signal, cotangent)
    return (*grads, fg.T)


def solution(mesh):
    spec = P("seq", "chan")
    return jax.shard_map(
        body, mesh=mesh, in_specs=(spec,) * 5, out_specs=(spec,) * 4, check_vma=False
    )
```

```python
import functools
import math

import jax
import jax.numpy as jnp
import numpy as np
import ml_dtypes
from jax import lax
from jax.experimental import pallas as pl
from jax.experimental.pallas import tpu as pltpu
from jax.sharding import PartitionSpec as P

BF = jnp.bfloat16
F32 = jnp.float32

N = 8192
A = 64
B = 128
SHARDS = 32
MEMBERS = 64
ROWS = 34
SCATTER = np.random.RandomState(10).permutation(SHARDS)
VMEM_LIMIT = 16 * 1024 * 1024


def two_parts(table):
    high = table.astype(ml_dtypes.bfloat16)
    low = (table - high.astype(np.float64)).astype(ml_dtypes.bfloat16)
    return high, low


def tables():
    order = np.array([2 * s + h for h in range(2) for s in SCATTER])
    k1 = np.arange(A) - 0.25
    angle1 = 2 * np.pi / A * np.outer(k1, order)
    w1 = np.concatenate([np.cos(angle1), -np.sin(angle1)], axis=0)
    high, low = two_parts(w1)
    w1cat = np.concatenate([high, high, low], axis=1)
    v1 = np.concatenate([np.cos(angle1), -np.sin(angle1)], axis=0).T / N
    high, low = two_parts(v1)
    v1cat = np.concatenate([high, high, low], axis=1)
    angle2 = 2 * np.pi / B * np.outer(np.arange(B), np.arange(B))
    c, s = np.cos(angle2), np.sin(angle2)
    w2 = np.block([[c, -s], [s, c]])
    w2h, w2l = two_parts(w2)
    angle = 2 * np.pi / N * np.outer(k1, np.arange(B))
    twiddle = np.stack([np.cos(angle), np.sin(angle)]).astype(np.float32)
    return w1cat, w2h, w2l, twiddle, v1cat


def split(x):
    high = x.astype(BF)
    return high, (x - high.astype(F32)).astype(BF)


def dot(x, y):
    return jnp.dot(x, y, preferred_element_type=F32)


def first_stage(columns, w1, c, s):
    high, low = split(jnp.concatenate(columns, axis=1))
    out = dot(w1, jnp.concatenate([high, low, high], axis=0))
    pairs = []
    for i in range(len(columns)):
        re = out[:A, i * B : (i + 1) * B]
        im = out[A:, i * B : (i + 1) * B]
        pairs.append((re * c + im * s, im * c - re * s))
    return pairs


def second_stage(pairs, high_table, low_table):
    stacked = jnp.concatenate([jnp.concatenate(p, axis=1) for p in pairs], axis=0)
    high, low = split(stacked)
    return dot(high, high_table) + dot(low, high_table) + dot(high, low_table)


def last_stage(blocks, v1, c, s):
    re, im = [], []
    for block in blocks:
        qi, qr = block[:, :B], block[:, B:]
        re.append(qr * c - qi * s)
        im.append(qr * s + qi * c)
    both = jnp.concatenate([jnp.concatenate(re, axis=1), jnp.concatenate(im, axis=1)], axis=0)
    high, low = split(both)
    vh, vl = v1[:, : 2 * A], v1[:, 4 * A :]
    return dot(v1[:, : 4 * A], jnp.concatenate([high, low], axis=0)) + dot(vl, high)


def forward(columns, w1, w2h, w2l, c, s):
    return second_stage(first_stage(columns, w1, c, s), w2h, w2l)


def prep_kernel(outer_hbm, inner_hbm, signal_hbm, cot_hbm, filt_hbm, send_ref,
                outer_ref, inner_ref, signal_ref, cot_ref, filt_ref, sems):
    def load(i, from_ref, to_ref, rows):
        copy = pltpu.make_async_copy(from_ref.at[rows], to_ref.at[rows], sems.at[i])
        copy.start()
        return copy

    halves = [pl.ds(0, B), pl.ds(B, B)]
    arrays = [(inner_hbm, inner_ref), (signal_hbm, signal_ref), (cot_hbm, cot_ref), (outer_hbm, outer_ref)]
    copies = [load(i * 4 + j, *pair, rows) for i, rows in enumerate(halves) for j, pair in enumerate(arrays)]
    last = load(8, filt_hbm, filt_ref, pl.ds(0, 64))

    pairs = partners()

    def place(block, first_row, h, k):
        turned = block.T
        for e in range(2):
            row = first_row + h * 8 + k * 2 + e
            send_ref[pl.ds(row, MEMBERS, stride=ROWS), :] = turned[e * 64 : (e + 1) * 64]

    for h in range(2):
        rows = slice(h * B, (h + 1) * B)
        for copy in copies[h * 4 : h * 4 + 4]:
            copy.wait()
        for k in range(4):
            cols = pl.ds(pl.multiple_of(pairs[k] * B, B), B)
            place(inner_ref[rows, cols].astype(F32) * signal_ref[rows, cols].astype(F32), 0, h, k)
            place(cot_ref[rows, cols].astype(F32) * outer_ref[rows, cols].astype(F32), 16, h, k)
    last.wait()
    for h in range(2):
        send_ref[pl.ds(32 + h, MEMBERS, stride=ROWS), :] = filt_ref[:, h * B : (h + 1) * B]


def partners():
    pair = lax.axis_index("chan") // 2
    beside = pair + 1 - 2 * lax.rem(pair, 2)
    return [pair, beside, lax.rem(pair + 2, 4), lax.rem(beside + 2, 4)]


def gather_rows(ref, q, row, step):
    return jnp.concatenate(
        [ref[pl.ds(q * 32 * ROWS + row + step * h, 32, stride=ROWS), :] for h in range(2)], axis=0
    )


def pick_kernel(recv_ref, w1_ref, w2h_ref, w2l_ref, tw_ref, v1_ref, out_ref):
    for q in range(2):
        out_ref[q] = gather_rows(recv_ref, q, 32, 1)


def spectra_kernel(recv_ref, w1_ref, w2h_ref, w2l_ref, tw_ref, v1_ref, u_ref, g_ref, *rest,
                   channels):
    c, s = tw_ref[0], tw_ref[1]
    count = len(channels)
    *fg_refs, prod_ref = rest
    fg_places = [(ref, i) for ref in fg_refs for i in range(ref.shape[0])]
    for f, channel in enumerate(channels):
        columns = [gather_rows(recv_ref, q, channel + base, 8) for base in (0, 16) for q in range(2)]
        spec = forward(columns, w1_ref[...], w2h_ref[...], w2l_ref[...], c, s)
        u_ref[f] = spec[: 2 * A]
        g_ref[f] = spec[2 * A :]
        ur, ui = spec[: 2 * A, :B], spec[: 2 * A, B:]
        gr, gi = spec[2 * A :, :B], spec[2 * A :, B:]
        pr = gr * ur + gi * ui
        pi = gi * ur - gr * ui
        prod_ref[f] = jnp.concatenate([pi[:A] + pi[A:], pr[:A] + pr[A:]], axis=1)
    high, low = split(prod_ref[...].reshape(count * A, 2 * B))
    mid = dot(high, w2h_ref[...]) + dot(low, w2h_ref[...]) + dot(high, w2l_ref[...])
    out = last_stage([mid[i * A : (i + 1) * A] for i in range(count)], v1_ref[...], c, s)
    for i in range(count):
        fg_ref, place = fg_places[i]
        fg_ref[place] = out[:, i * B : (i + 1) * B]


def mix_kernel(near_ref, came_ref, give_ref):
    give_ref[...] = near_ref[2:4] + came_ref[...]


def conv_part(ks, filts, u_ref, g_ref, starts, w1, w2h, w2l, tw_ref, v1, out_ref):
    c, s = tw_ref[0], tw_ref[1]
    spec = forward([filt[q] for filt in filts for q in range(2)], w1, w2h, w2l, c, s)
    prods, places = [], []
    for j, k in enumerate(ks):
        for e in range(2):
            f = 2 * k + e
            at = starts[j] + e
            h_spec = spec[(2 * j + e) * A : (2 * j + e + 1) * A]
            hr, hi = h_spec[:, :B], h_spec[:, B:]
            for q in range(2):
                ur, ui = u_ref[at, q * A : (q + 1) * A, :B], u_ref[at, q * A : (q + 1) * A, B:]
                prods.append((hr * ui + hi * ur, hr * ur - hi * ui))
                places.append((q, f))
            for q in range(2):
                gr, gi = g_ref[at, q * A : (q + 1) * A, :B], g_ref[at, q * A : (q + 1) * A, B:]
                prods.append((gi * hr - gr * hi, gr * hr + gi * hi))
                places.append((q, 16 + f))
    mid = second_stage(prods, w2h, w2l)
    for n in range(0, len(prods), 4):
        out = last_stage([mid[i * A : (i + 1) * A] for i in range(n, n + 4)], v1, c, s)
        for i in range(4):
            q, row = places[n + i]
            for h in range(2):
                out_ref[pl.ds(q * 32 * ROWS + row + 8 * h, 32, stride=ROWS), :] = (
                    out[h * 32 : (h + 1) * 32, i * B : (i + 1) * B]
                )


def conv_three_kernel(own_ref, fb_ref, fa_ref, u_ref, g_ref, w1_ref, w2h_ref, w2l_ref, tw_ref, v1_ref,
                      out_ref):
    conv_part((0, 1, 3), (own_ref, fb_ref, fa_ref), u_ref, g_ref, (2, 4, 0), w1_ref[...], w2h_ref[...],
              w2l_ref[...], tw_ref, v1_ref[...], out_ref)


def conv_last_kernel(far_ref, base_ref, u_ref, g_ref, w1_ref, w2h_ref, w2l_ref, tw_ref, v1_ref, out_ref):
    out_ref[...] = base_ref[...]
    conv_part((2,), (far_ref,), u_ref, g_ref, (0,), w1_ref[...], w2h_ref[...], w2l_ref[...], tw_ref,
              v1_ref[...], out_ref)


def place_kernel(near_ref, direct_ref, came_ref, base_ref, out_ref):
    out_ref[...] = base_ref[...]
    for q in range(2):
        total = near_ref[q] + direct_ref[q] + came_ref[q]
        for h in range(2):
            out_ref[pl.ds(q * 32 * ROWS + 32 + h, 32, stride=ROWS), :] = total[h * 32 : (h + 1) * 32]


def post_kernel(recv_ref, inner_ref, signal_ref, cot_ref, og_hbm, ig_hbm, sg_hbm, fg_hbm,
                og_ref, ig_ref, sg_ref, fg_ref, sems):
    pairs = partners()

    def fetch(first_row, h, k):
        blocks = [
            recv_ref[pl.ds(first_row + h * 8 + k * 2 + e, MEMBERS, stride=ROWS), :] for e in range(2)
        ]
        return jnp.concatenate(blocks, axis=0).T

    copies = []

    def store(from_ref, to_ref, rows):
        copy = pltpu.make_async_copy(from_ref.at[rows], to_ref.at[rows], sems.at[len(copies)])
        copy.start()
        copies.append(copy)

    for h in range(2):
        block = recv_ref[pl.ds(32 + h, MEMBERS, stride=ROWS), :]
        fg_ref[:, h * B : (h + 1) * B] = block * (1.0 / math.sqrt(N))
    store(fg_ref, fg_hbm, pl.ds(0, 64))
    for h in range(2):
        rows = slice(h * B, (h + 1) * B)
        for k in range(4):
            cols = pl.ds(pl.multiple_of(pairs[k] * B, B), B)
            back = fetch(16, h, k)
            ig_ref[rows, cols] = (back * signal_ref[rows, cols].astype(F32)).astype(BF)
            sg_ref[rows, cols] = (back * inner_ref[rows, cols].astype(F32)).astype(BF)
        store(ig_ref, ig_hbm, pl.ds(h * B, B))
        store(sg_ref, sg_hbm, pl.ds(h * B, B))
    for h in range(2):
        rows = slice(h * B, (h + 1) * B)
        for k in range(4):
            cols = pl.ds(pl.multiple_of(pairs[k] * B, B), B)
            og_ref[rows, cols] = (cot_ref[rows, cols].astype(F32) * fetch(0, h, k)).astype(BF)
        store(og_ref, og_hbm, pl.ds(h * B, B))
    for copy in copies:
        copy.wait()


def call(kernel, out_shapes, name, scratch=(), cost=(1000, 1000), ins=None, outs=None):
    return pl.pallas_call(
        kernel,
        out_shape=out_shapes,
        in_specs=pl.no_block_spec if ins is None else ins,
        scratch_shapes=list(scratch),
        name=name,
        out_specs=pl.no_block_spec if outs is None else outs,
        compiler_params=pltpu.CompilerParams(vmem_limit_bytes=VMEM_LIMIT),
        cost_estimate=pl.CostEstimate(flops=cost[0], bytes_accessed=cost[1], transcendentals=0),
    )


def shape(*dims, dtype=F32):
    return jax.ShapeDtypeStruct(dims, dtype)


PAIRS = [[s * 8 + 2 * p + q for q in range(2) for s in SCATTER.tolist()] for p in range(4)]


def exchange(x):
    x = x.reshape(MEMBERS, ROWS * B)
    x = lax.all_to_all(x, ("seq", "chan"), 0, 0, axis_index_groups=PAIRS, tiled=True)
    return x.reshape(MEMBERS * ROWS, B)


def swap(x, distance):
    return lax.ppermute(x, "chan", [(z, z ^ distance) for z in range(8)])


def body(outer_gate, inner_gate, signal, cotangent, filters):
    w1, w2h, w2l, tw, v1 = [jnp.asarray(t) for t in tables()]
    buffer = shape(MEMBERS * ROWS, B)
    two = shape(2, A, B)
    gate = pltpu.VMEM((256, 512), BF)
    send = call(
        prep_kernel, buffer, "prep",
        [gate, gate, gate, gate, pltpu.VMEM((64, 256), F32), pltpu.SemaphoreType.DMA((9,))],
        ins=[pl.BlockSpec(memory_space=pltpu.HBM)] * 5,
    )(*[
        pltpu.with_memory_space_constraint(x, pltpu.HBM)
        for x in (outer_gate, inner_gate, signal, cotangent, filters.T)
    ])
    recv = exchange(send)
    tables_in = (w1, w2h, w2l, tw, v1)
    own = call(pick_kernel, two, "pick")(recv, *tables_in)
    fa, fb = swap(own, 6), swap(own, 2)
    def spectra(recv, ks, sizes):
        channels = [2 * k + e for k in ks for e in range(2)]
        count = len(channels)
        return call(
            functools.partial(spectra_kernel, channels=channels),
            (shape(count, 2 * A, 2 * B), shape(count, 2 * A, 2 * B))
            + tuple(shape(size, A, B) for size in sizes),
            "spectra",
            [pltpu.VMEM((count, A, 2 * B), F32)],
            (1000, 1000),
        )(recv, *tables_in)

    ur, gr, relay = spectra(recv, (2,), (2,))
    recv, relay = lax.optimization_barrier((recv, relay))
    relay = swap(relay, 6)
    un, gn, direct, near = spectra(recv, (3, 0, 1), (2, 4))
    fb, near = lax.optimization_barrier((fb, near))
    far = swap(fb, 6)
    direct = swap(direct, 6)
    three = call(conv_three_kernel, buffer, "three", cost=(1000, 1000))(
        own, fb, fa, un, gn, *tables_in
    )
    came = swap(call(mix_kernel, two, "mix")(near, relay), 2)
    last = call(conv_last_kernel, buffer, "last", cost=(1000, 1000))(far, three, ur, gr, *tables_in)
    back_send = call(place_kernel, buffer, "place")(near, direct, came, last)
    landed = exchange(back_send)
    *grads, fg = call(
        post_kernel,
        (shape(256, 512, dtype=BF), shape(256, 512, dtype=BF), shape(256, 512, dtype=BF), shape(64, 256)),
        "post",
        [gate, gate, gate, pltpu.VMEM((64, 256), F32), pltpu.SemaphoreType.DMA((7,))],
        outs=[pl.BlockSpec(memory_space=pltpu.HBM)] * 4,
    )(landed, inner_gate, signal, cotangent)
    return (*grads, fg.T)


def solution(mesh):
    spec = P("seq", "chan")
    return jax.shard_map(
        body, mesh=mesh, in_specs=(spec,) * 5, out_specs=(spec,) * 4, check_vma=False
    )
```
